128 devices in a mesh: section: 4 (over x), expert: 16 (over y, z_lo, core), dp: 2 (over z_hi).
Axes of the slice: x: 4, y: 4, z: 4 (z_hi: 2, z_lo: 2; z = z_hi * 2 + z_lo), core: 2. Of those that a mesh axis runs over, the one named last changes fastest.
Arguments:
- tokens: bfloat16 [4, 2, 2048, 3584], P('section', 'dp', 'expert'), may hold values from -6 to 6
- grad_out: bfloat16 [4, 2, 2048, 3584], P('section', 'dp', 'expert'), may hold values from -6 to 6
- expert_ids: int32 [4, 2, 2048, 2], P('section', 'dp', 'expert'), may hold values from 0 to 15, all different within a row; in each aligned block of 128 rows (0 to 127, 128 to 255, ..., all dimensions but the last counted through in order) at most 24 rows name the same one
- route_weight: float32 [4, 2, 2048, 2], P('section', 'dp', 'expert'), may hold values from 0.1 to 1
- w_gate: bfloat16 [4, 16, 3584, 1024], P('section', 'expert', None, 'dp'), may hold values from -0.09375 to 0.09375
- w_up: bfloat16 [4, 16, 3584, 1024], P('section', 'expert', None, 'dp'), may hold values from -0.09375 to 0.09375
- w_down: bfloat16 [4, 16, 1024, 3584], P('section', 'expert', 'dp'), may hold values from -0.1875 to 0.1875
Outputs:
- next_input: bfloat16 [4, 2, 2048, 3584], P('section', 'dp', 'expert')
- prev_grad: bfloat16 [4, 2, 2048, 3584], P('section', 'dp', 'expert')
- grad_gate: bfloat16 [4, 16, 3584, 1024], P('section', 'expert', None, 'dp')
- grad_up: bfloat16 [4, 16, 3584, 1024], P('section', 'expert', None, 'dp')
- grad_down: bfloat16 [4, 16, 1024, 3584], P('section', 'expert', 'dp')
The draws below stay inside these ranges and needn't reach their ends.
Inputs may be any that keep to these rules, and one draw needn't show every extreme that they name: `expert_ids`: each row names 2 different experts; within each aligned block of 128 rows (the rows of one device) no expert is named more than 24 times, a bound that some block reaches.
All inputs are finite; a program needn't handle non-finite values.
Results may differ from the reference program's by a relative error of at most 0.0065.
Values may be sent and summed in bfloat16 or wider, within the bound.
No kernel may reach another device: no remote copies, remote signals or barrier semaphores. Data moves between devices by JAX's collectives and lax.ppermute only.
A program may use at most 192 MiB of HBM per device.

```python
import math
import jax
import jax.numpy as jnp
import numpy as np
from jax import lax

D = 3584
FF = 1024
TOPK = 2
TOK_DEV = 128
EXPERTS = 16
SECTIONS = 4
REPLICAS = 2
TOKENS = 2048
SLOT = 24


def levels(stream_key, shape, cuts, smallest, largest):
    def one(axis_at, blocks):
        steps = jax.random.uniform(jax.random.fold_in(jax.random.fold_in(stream_key, 6), axis_at), (blocks,), jnp.float32, smallest / len(cuts), largest / len(cuts))
        return jnp.repeat(jnp.exp(steps), shape[axis_at] // blocks).reshape((-1,) + (1,) * (len(shape) - axis_at - 1))

    level = one(*cuts[0])
    for cut in cuts[1:]:
        level = level * one(*cut)
    return level


def shared_out(stream_key, own, number, rows, number_of, top, most, lean):
    sequence = jax.random.permutation(stream_key, number_of)
    packed, common = load_shares(number_of, rows * top, most, lean, True), load_shares(number_of, rows * top, most, lean, False)
    places = jnp.arange(number_of)

    def named(tallies, rotation):
        used = int((tallies > 0).sum())
        fixed = max(1, used // 4)
        passed = fixed + (places - fixed + rotation * (used - fixed)) % max(1, number_of - fixed)
        return jnp.zeros((number_of,), jnp.int32).at[sequence[jnp.where(places < fixed, places, passed)]].set(jnp.asarray(tallies, jnp.int32))

    tallies = jnp.where(number % 4 == 0, named(packed, number // 4), named(common, number - number // 4 - 1))
    mixed = jax.random.permutation(jax.random.fold_in(own, 3), number_of)
    source_of, receiver = mixed[0:number_of // 2 * 2:2], mixed[1:number_of // 2 * 2:2]
    room = jnp.minimum(tallies[source_of] - 1, most - tallies[receiver]) // 2
    room = jnp.where((source_of == sequence[0]) | (receiver == sequence[0]) | (tallies[receiver] == 0), 0, jnp.maximum(room, 0))
    passed = jax.random.randint(jax.random.fold_in(own, 4), (number_of // 2,), 0, 1 << 20) % (room + 1)
    tallies = tallies.at[source_of].add(-passed).at[receiver].add(passed)
    items = jnp.searchsorted(jnp.cumsum(tallies), jnp.arange(rows * top), side="right").astype(jnp.int32)
    table = items.reshape(top, rows).T
    table = table[jax.random.permutation(jax.random.fold_in(own, 1), rows)]
    rotation = jax.random.randint(jax.random.fold_in(own, 2), (rows, 1), 0, top)
    return jnp.take_along_axis(table, (jnp.arange(top)[None, :] + rotation) % top, axis=1)


def load_shares(amount, total, most, slope, full):
    portions = [(1 << 20) // math.isqrt(standing ** slope) + 1 for standing in range(1, amount + 1)]
    largest = most if full else min(most, max(-(-total // amount), total * portions[0] // sum(portions)))
    least = 1 if total - largest >= amount - 1 else 0
    counts, rest = [largest] + [least] * (amount - 1), total - largest - least * (amount - 1)
    while rest > 0:
        movable = [i for i in range(1, amount) if counts[i] < largest] or [i for i in range(1, amount) if counts[i] < most]
        whole, remaining = sum([portions[i] for i in movable]), rest
        for i in movable:
            extra = min(most - counts[i], max(1, remaining * portions[i] // whole), rest)
            counts[i] = counts[i] + extra
            rest = rest - extra
    return np.array(counts)


def noise(own_key, shape, scale, bound, split=(), kind=jnp.bfloat16):
    array = jax.random.normal(own_key, shape, jnp.float32) * scale
    if len(split) > 0:
        array = levels(own_key, shape, split, -0.22, 0.18) * array
    return jnp.clip(array, min=-bound, max=bound).astype(kind)


def setup_inputs(seed: int = 0) -> dict:
    keys = jax.random.split(jax.random.key(seed), 8)
    tokens = noise(keys[0], (SECTIONS, REPLICAS, TOKENS, D), 1.0, 6.0, ((0, 4), (1, 2), (2, 16)))
    grad_out = noise(keys[1], (SECTIONS, REPLICAS, TOKENS, D), 1.0, 6.0, ((0, 4), (1, 2), (2, 16)))
    expert_ids_keys = jax.random.split(jax.random.fold_in(keys[2], 1), SECTIONS * REPLICAS * TOKENS // TOK_DEV)
    expert_ids_turns = jax.random.permutation(jax.random.fold_in(keys[2], 3), SECTIONS * REPLICAS * TOKENS // TOK_DEV)
    expert_ids = jax.vmap(lambda own, number: shared_out(jax.random.fold_in(keys[2], 2), own, number, TOK_DEV, EXPERTS, TOPK, SLOT, 2))(expert_ids_keys, expert_ids_turns).reshape((SECTIONS, REPLICAS, TOKENS, TOPK))
    route_weight = jnp.clip(jnp.exp(math.log(1.0) - 2.3025851 * jax.random.uniform(keys[3], (SECTIONS, REPLICAS, TOKENS, TOPK), jnp.float32) ** levels(keys[3], (SECTIONS, REPLICAS, TOKENS, TOPK), ((0, 4), (1, 2), (2, 16)), -0.2, 0.2)), 0.1, 1.0)
    w_gate = noise(keys[4], (SECTIONS, EXPERTS, D, FF), D ** -0.5, 0.09375, ((0, 4), (1, 16), (3, 2)))
    w_up = noise(keys[5], (SECTIONS, EXPERTS, D, FF), D ** -0.5, 0.09375, ((0, 4), (1, 16), (3, 2)))
    w_down = noise(keys[6], (SECTIONS, EXPERTS, FF, D), FF ** -0.5, 0.1875, ((0, 4), (1, 16), (2, 2)))
    return dict(tokens=tokens, grad_out=grad_out, expert_ids=expert_ids, route_weight=route_weight, w_gate=w_gate, w_up=w_up, w_down=w_down)


def slot_table(routed, replica):
    blocks = routed.reshape(EXPERTS, TOK_DEV * TOPK)
    onehot = (blocks[:, :, None] == jnp.arange(EXPERTS, dtype=jnp.int32)[None, None, :]).astype(jnp.int32)
    earlier = jnp.cumsum(onehot, axis=1) - 1
    position = jnp.sum(earlier * onehot, axis=2)
    source = jnp.arange(EXPERTS, dtype=jnp.int32)[:, None]
    table = replica * (EXPERTS * SLOT) + source * SLOT + position
    return table.reshape(TOKENS, TOPK).astype(jnp.int32)


def expert_pass(operands):
    inputs, cotangents, gate_matrix, up_matrix, down_matrix = operands
    gate_pre = jnp.dot(inputs, gate_matrix, preferred_element_type=jnp.float32)
    up_pre = jnp.dot(inputs, up_matrix, preferred_element_type=jnp.float32)
    sigmoid_gate = jax.nn.sigmoid(gate_pre)
    hidden = (gate_pre * sigmoid_gate * up_pre).astype(jnp.bfloat16)
    result = jnp.dot(hidden, down_matrix, preferred_element_type=jnp.float32).astype(jnp.bfloat16)
    hidden_grad = jnp.dot(cotangents, down_matrix.T, preferred_element_type=jnp.float32)
    gate_grad = (hidden_grad * up_pre * sigmoid_gate * (1.0 + gate_pre * (1.0 - sigmoid_gate))).astype(jnp.bfloat16)
    up_grad = (hidden_grad * gate_pre * sigmoid_gate).astype(jnp.bfloat16)
    down_total = jnp.dot(hidden.T, cotangents, preferred_element_type=jnp.float32).astype(jnp.bfloat16)
    gate_total = jnp.dot(inputs.T, gate_grad, preferred_element_type=jnp.float32).astype(jnp.bfloat16)
    up_total = jnp.dot(inputs.T, up_grad, preferred_element_type=jnp.float32).astype(jnp.bfloat16)
    back_rows = (jnp.dot(gate_grad, gate_matrix.T, preferred_element_type=jnp.float32)
                 + jnp.dot(up_grad, up_matrix.T, preferred_element_type=jnp.float32)).astype(jnp.bfloat16)
    return result, back_rows, gate_total, up_total, down_total


def reference(tokens, grad_out, expert_ids, route_weight, w_gate, w_up, w_down):
    mixed_all, input_all = [], []
    gate_all, up_all, down_all = [], [], []
    buffer_rows = REPLICAS * EXPERTS * SLOT
    for section_index in range(SECTIONS):
        inputs = jnp.zeros((EXPERTS, buffer_rows, D), jnp.bfloat16)
        cotangents = jnp.zeros((EXPERTS, buffer_rows, D), jnp.bfloat16)
        tables = []
        for replica in range(REPLICAS):
            routed = expert_ids[section_index, replica]
            table = slot_table(routed, replica)
            weights = route_weight[section_index, replica].astype(jnp.float32)
            spread = jnp.broadcast_to(tokens[section_index, replica][:, None, :], (TOKENS, TOPK, D))
            scaled = (weights[:, :, None] * grad_out[section_index, replica][:, None, :].astype(jnp.float32)).astype(jnp.bfloat16)
            inputs = inputs.at[routed, table].set(spread)
            cotangents = cotangents.at[routed, table].set(scaled)
            tables.append(table)
        result, back_rows, gate_total, up_total, down_total = lax.map(
            expert_pass, (inputs, cotangents, w_gate[section_index], w_up[section_index], w_down[section_index]))
        mixed_section, input_section = [], []
        for replica in range(REPLICAS):
            routed = expert_ids[section_index, replica]
            table = tables[replica]
            weights = route_weight[section_index, replica].astype(jnp.float32)
            picked = result[routed, table].astype(jnp.float32)
            mixed_section.append(jnp.sum(weights[:, :, None] * picked, axis=1).astype(jnp.bfloat16))
            returned = back_rows[routed, table].astype(jnp.float32)
            input_section.append(jnp.sum(returned, axis=1).astype(jnp.bfloat16))
        mixed_all.append(jnp.stack(mixed_section))
        input_all.append(jnp.stack(input_section))
        gate_all.append(gate_total)
        up_all.append(up_total)
        down_all.append(down_total)
    zero_block = jnp.zeros((REPLICAS, TOKENS, D), jnp.bfloat16)
    next_input = jnp.stack([zero_block] + mixed_all[:-1])
    prev_grad = jnp.stack(input_all[1:] + [zero_block])
    return next_input, prev_grad, jnp.stack(gate_all), jnp.stack(up_all), jnp.stack(down_all)
```

```python
import jax
import jax.numpy as jnp
from jax import lax
from jax.experimental import pallas as pl
from jax.experimental.pallas import tpu as pltpu
from jax.sharding import PartitionSpec as P

GROUP = ("expert", "dp")
BF = jnp.bfloat16
F32 = jnp.float32


def place(y, z, c):
    return (((y * 2 + z % 2) * 2 + c) * 2) + z // 2


def shifted(x, dy, dz, dc):
    pairs = [
        (place(y, z, c), place((y + dy) % 4, (z + dz) % 4, c ^ dc))
        for y in range(4)
        for z in range(4)
        for c in range(2)
    ]
    return lax.ppermute(x, GROUP, pairs)


def shift_y(x, by):
    return x if by % 4 == 0 else shifted(x, by, 0, 0)


def shift_z(x, by):
    return x if by % 4 == 0 else shifted(x, 0, by, 0)


def swap_core(x):
    return shifted(x, 0, 0, 1)


def after(x, done):
    return lax.optimization_barrier((x, done))[0]


def from_behind(x, axis, by):
    count = lax.axis_size(axis)
    pairs = [(i, i + by) for i in range(count) if 0 <= i + by < count]
    return lax.ppermute(x, axis, pairs)


def slot_codes(ids, experts, slot_rows):
    rows = ids.shape[-2]
    onehot = (ids[..., None] == jnp.arange(experts, dtype=F32)).astype(F32)
    named = jnp.sum(onehot, axis=-2).astype(BF)
    before = jnp.tri(rows, k=-1, dtype=BF)
    earlier = jnp.einsum("ij,...je->...ie", before, named, preferred_element_type=F32)
    position = jnp.sum(onehot * earlier[..., None, :], axis=-1)
    return (ids * slot_rows + position).astype(jnp.int32)


def chosen(codes, weights, targets):
    hits = [codes[..., k, None] == targets for k in range(codes.shape[-1])]
    weight = sum(jnp.sum(jnp.where(h, weights[..., k, None], 0.0), axis=-2) for k, h in enumerate(hits))
    return [h.astype(BF) for h in hits], hits[0].astype(BF) + hits[1].astype(BF), weight


def in_three(w):
    high = lax.reduce_precision(w, 8, 7)
    middle = lax.reduce_precision(w - high, 8, 7)
    return high, middle, w - high - middle


def mm(a, b):
    return jnp.dot(a, b, preferred_element_type=F32)


def mm_last(a, b):
    return lax.dot_general(a, b, (((1,), (1,)), ((), ())), preferred_element_type=F32)


def mm_first(a, b):
    return lax.dot_general(a, b, (((0,), (0,)), ((), ())), preferred_element_type=F32)


def kernel_call(body, grid, in_specs, out_specs, out_shape, scratch=()):
    return pl.pallas_call(
        body,
        grid=(grid,),
        in_specs=in_specs,
        out_specs=out_specs,
        out_shape=out_shape,
        scratch_shapes=scratch,
        compiler_params=pltpu.CompilerParams(vmem_limit_bytes=40 * 1024 * 1024),
        cost_estimate=pl.CostEstimate(flops=1, bytes_accessed=1, transcendentals=0),
    )


def whole(x):
    return pl.BlockSpec(x.shape, lambda i: (0, 0))


def columns(rows, n):
    return pl.BlockSpec((rows, n), lambda i: (0, i))


def rows_block(n, width):
    return pl.BlockSpec((n, width), lambda i: (i, 0))


def forward(pieces, gate_matrix, up_matrix):
    count, rows = len(pieces), pieces[0].shape[0]
    depth, units = gate_matrix.shape
    n = units // 2

    def body(*refs):
        gate, up, outs = refs[count], refs[count + 1], refs[count + 2 :]
        for i in range(count):
            x = refs[i][...]
            g, u = mm(x, gate[...]), mm(x, up[...])
            outs[3 * i][...] = g
            outs[3 * i + 1][...] = u
            outs[3 * i + 2][...] = (g * jax.nn.sigmoid(g) * u).astype(BF)

    shapes = [jax.ShapeDtypeStruct((rows, units), t) for t in (F32, F32, BF)] * count
    outs = kernel_call(
        body,
        2,
        [whole(x) for x in pieces] + [columns(depth, n)] * 2,
        [columns(rows, n)] * (3 * count),
        shapes,
    )(*pieces, gate_matrix, up_matrix)
    return [outs[3 * i : 3 * i + 3] for i in range(count)]


def outputs(hidden, down_matrix):
    count, rows = len(hidden), hidden[0].shape[0]
    units, width = down_matrix.shape
    n = width // 7

    def body(*refs):
        for i in range(count):
            refs[count + 1 + i][...] = mm(refs[i][...], refs[count][...]).astype(BF)

    return kernel_call(
        body,
        7,
        [whole(h) for h in hidden] + [columns(units, n)],
        [columns(rows, n)] * count,
        [jax.ShapeDtypeStruct((rows, width), BF)] * count,
    )(*hidden, down_matrix)


def hidden_grads(pieces, down_matrix):
    count, rows = len(pieces), pieces[0].shape[0]
    units, width = down_matrix.shape
    n = units // 2

    def body(*refs):
        for i in range(count):
            refs[count + 1 + i][...] = mm_last(refs[i][...], refs[count][...])

    return kernel_call(
        body,
        2,
        [whole(g) for g in pieces] + [rows_block(n, width)],
        [columns(rows, n)] * count,
        [jax.ShapeDtypeStruct((rows, units), F32)] * count,
    )(*pieces, down_matrix)


def backward(groups, slot, gate_pre, up_pre, hidden_grad, gate_matrix, up_matrix):
    used_s = sorted({s for _, those in groups for s in those})
    pairs = sorted((s, t) for t, those in groups for s in those)
    rows, units = gate_pre[used_s[0]].shape
    width = gate_matrix.shape[0]
    n = width // 7
    counts = [2 * len(those) * slot for _, those in groups]
    starts = [sum(counts[:i]) for i in range(len(groups))]
    total = sum(counts)
    many, those_s = len(groups), len(used_s)

    def body(*refs):
        gates = dict(zip(used_s, refs[:those_s]))
        ups = dict(zip(used_s, refs[those_s : 2 * those_s]))
        refs = refs[2 * those_s :]
        grads, (gate, up), refs = refs[:many], refs[many : many + 2], refs[many + 2 :]
        backs, (gate_out, up_out, gate_rows, up_rows) = refs[:many], refs[many:]

        @pl.when(pl.program_id(0) == 0)
        def _():
            for i, (t, those) in enumerate(groups):
                terms = {}
                for d in range(2):
                    for s in those:
                        here = pl.ds((t * 2 + d) * slot, slot)
                        g, u = gates[s][here, :], ups[s][here, :]
                        h = grads[i][pl.ds((d * 4 + s) * slot, slot), :]
                        sig = jax.nn.sigmoid(g)
                        terms[d, s] = (h * u * sig * (1.0 + g * (1.0 - sig)), h * g * sig)
                order = [terms[d, s] for d in range(2) for s in those]
                for which, by_t, by_s in ((0, gate_rows, gate_out), (1, up_rows, up_out)):
                    for k in range(0, len(order), 2):
                        pair = jnp.concatenate([order[k][which], order[k + 1][which]], axis=0)
                        by_t[pl.ds(starts[i] + k * slot, 2 * slot), :] = pair.astype(BF)
                    for s in those:
                        pair = jnp.concatenate([terms[0, s][which], terms[1, s][which]], axis=0)
                        by_s[pl.ds(pairs.index((s, t)) * 2 * slot, 2 * slot), :] = pair.astype(BF)

        back = mm_last(gate_rows[...], gate[...]) + mm_last(up_rows[...], up[...])
        for i in range(many):
            backs[i][...] = back[starts[i] : starts[i] + counts[i]].astype(BF)

    both = jax.ShapeDtypeStruct((total, units), BF)
    operands = [gate_pre[s] for s in used_s] + [up_pre[s] for s in used_s]
    operands += [hidden_grad[t] for t, _ in groups]
    outs = kernel_call(
        body,
        7,
        [whole(a) for a in operands] + [rows_block(n, units)] * 2,
        [columns(count, n) for count in counts] + [whole(both)] * 2,
        [jax.ShapeDtypeStruct((count, width), BF) for count in counts] + [both] * 2,
        [pltpu.VMEM(both.shape, BF)] * 2,
    )(*operands, gate_matrix, up_matrix)
    grads = [
        {pair: a[k * 2 * slot : (k + 1) * 2 * slot] for k, pair in enumerate(pairs)} for a in outs[many:]
    ]
    return outs[:many], grads[0], grads[1]


def local(tokens, grad_out, expert_ids, route_weight, w_gate, w_up, w_down):
    inputs = tokens[0, 0]
    upstream = grad_out[0, 0]
    weights = route_weight[0, 0]
    gate_matrix, up_matrix, down_matrix = w_gate[0, 0], w_up[0, 0], w_down[0, 0]
    experts = lax.axis_size("expert")
    rows, per_token = weights.shape
    width = inputs.shape[1]
    half = width // 2
    slot = 3 * rows * per_token // (2 * experts)
    flat = 8 * slot
    me = lax.axis_index("expert")
    y, zl, c = me // 4, (me // 2) % 2, me % 2

    ids = expert_ids[0, 0].astype(F32)
    fields = [ids] + [jnp.stack([a[:, k] for a in in_three(weights)], axis=1) for k in range(per_token)]
    fields = jnp.concatenate(fields, axis=1).astype(BF)
    table = jnp.pad(fields, ((0, 0), (0, 128 - fields.shape[1])))
    message = jnp.concatenate([upstream, table], axis=1)
    near1, near3 = shift_z(message, 1), shift_z(message, 3)
    codes = slot_codes(ids, experts, slot)
    step = jnp.arange(4, dtype=jnp.int32)
    two = jnp.arange(2, dtype=jnp.int32)
    slots = jnp.arange(slot, dtype=jnp.int32)
    dest_y = ((y + step) % 4) * 4
    targets_z = (
        (dest_y[None, :, None] + zl * 2 + (c ^ two)[:, None, None]) * slot + slots
    ).reshape(-1)
    targets_y = (
        (
            dest_y[None, :, None, None]
            + (zl ^ two)[None, None, :, None] * 2
            + (c ^ two)[:, None, None, None]
        )
        * slot
        + slots
    ).reshape(-1)
    each_y, pick_y, _ = chosen(codes, weights, targets_y)
    own, sib = [
        mm_first(pick_y[:, dc * flat : (dc + 1) * flat], inputs).astype(BF).reshape(4, 2, slot, width)
        for dc in range(2)
    ]
    sib = swap_core(sib)
    along_y = [jnp.stack([own[t], sib[t]]) for t in range(4)]
    y1, y3 = shift_y(along_y[1], 1), shift_y(along_y[3], 3)

    near1, near3, y1, y3, far_y = lax.optimization_barrier((near1, near3, y1, y3, along_y[2]))
    y2 = shift_y(far_y, 2)
    far_a, far_b = shift_z(near1[:, :half], 1), shift_z(near3[:, half:], 3)

    def picks(tables):
        tables = tables.astype(F32)
        chose = tables[..., :per_token]
        parts = [tables[..., per_token + 3 * k : per_token + 3 * k + 3] for k in range(per_token)]
        weigh = jnp.stack([p[..., 0] + p[..., 1] + p[..., 2] for p in parts], axis=-1)
        return chosen(slot_codes(chose, experts, slot), weigh, targets_z)[1:]

    tables = jnp.stack([fields, near1[:, width : width + 8], near3[:, width : width + 8]])
    pick_z, slot_weight_z = picks(tables)
    pick_z = {0: pick_z[0], 1: pick_z[1], 3: pick_z[2]}

    def select(pick, weight, block):
        return (weight[:, None] * mm_first(pick, block)).astype(BF).reshape(2, 4, slot, width)

    sel = {
        0: select(pick_z[0], slot_weight_z[0], upstream),
        1: select(pick_z[1], slot_weight_z[1], near1[:, :width]),
        3: select(pick_z[3], slot_weight_z[2], near3[:, :width]),
    }
    swapped = swap_core(jnp.stack([sel[0][1], sel[1][1], sel[3][1]]))

    pick_z[2], weight_far = picks(far_b[:, width - half : width - half + 8])
    sel[2] = select(pick_z[2], weight_far, jnp.concatenate([far_a, far_b[:, : width - half]], axis=1))

    sel[2], y1, y2, y3, swapped = lax.optimization_barrier((sel[2], y1, y2, y3, swapped))
    by_y = [along_y[0], y1, y2, y3]
    same, other = [jnp.stack([a[:, dl] for a in by_y]).reshape(flat, width) for dl in range(2)]
    x1, x3 = shift_z(other, 1), shift_z(other, 3)
    sib = [swapped[0], swapped[1], swap_core(sel[2][1]), swapped[2]]
    out_y = [
        jnp.stack([sel[s][0][t] for s in range(4)] + [a[t] for a in sib]).reshape(flat, width)
        for t in range(4)
    ]
    g1, g3 = shift_y(out_y[1], 1), shift_y(out_y[3], 3)

    x1, x3, g1, g3, same_far, out_far = lax.optimization_barrier((x1, x3, g1, g3, same, out_y[2]))
    x2, g2 = shift_z(same_far, 2), shift_y(out_far, 2)
    ahead = forward([x1, x3, same_far], gate_matrix, up_matrix)
    out1, out3 = outputs([ahead[0][2], ahead[1][2]], down_matrix)
    grad1, grad3, grad0 = hidden_grads([g1, g3, out_y[0]], down_matrix)
    gate_pre, up_pre, hidden = [{0: ahead[2][i], 1: ahead[0][i], 3: ahead[1][i]} for i in range(3)]
    early = ((1, (0, 1, 3)), (3, (0, 1, 3)))
    (back1, back3), gate_grad, up_grad = backward(
        early, slot, gate_pre, up_pre, {1: grad1, 3: grad3}, gate_matrix, up_matrix
    )

    x2, g2, out1, out3, back1, back3 = lax.optimization_barrier((x2, g2, out1, out3, back1, back3))
    e1, e3 = shift_z(out1, -1), shift_z(out3, -3)
    b1, b3 = shift_y(back1, -1), shift_y(back3, -3)
    ((gate_pre[2], up_pre[2], hidden[2]),) = forward([x2], gate_matrix, up_matrix)
    (grad2,) = hidden_grads([g2], down_matrix)
    out2, out0 = outputs([hidden[2], hidden[0]], down_matrix)
    rest = ((0, (0, 1, 2, 3)), (2, (0, 1, 2, 3)), (1, (2,)), (3, (2,)))
    (back0, back2, back1, back3), more_gate, more_up = backward(
        rest,
        slot,
        gate_pre,
        up_pre,
        {0: grad0, 1: grad1, 2: grad2, 3: grad3},
        gate_matrix,
        up_matrix,
    )
    gate_grad, up_grad = {**gate_grad, **more_gate}, {**up_grad, **more_up}

    e1, e3, b1, b3, out0, out2, back0, back1, back2, back3 = lax.optimization_barrier(
        (e1, e3, b1, b3, out0, out2, back0, back1, back2, back3)
    )
    e2, b2 = shift_z(out2, -2), shift_y(back2, -2)
    far1, far3 = shift_y(back1, -1), shift_y(back3, -3)
    back0 = back0.reshape(2, 4, slot, width)
    b1, b3 = [a.reshape(2, 3, slot, width) for a in (b1, b3)]
    swapped = swap_core(jnp.concatenate([back0[1], b1[1], b3[1]]))
    late_g, late_hidden, _ = lax.optimization_barrier(((out_y[0], g1, g2, g3), hidden, e1))
    late_hidden = jnp.stack([late_hidden[s].reshape(4, 2, slot, -1) for s in range(4)], axis=2)
    down_total = mm_first(late_hidden.reshape(4 * flat, -1), jnp.concatenate(late_g)).astype(BF)

    e2, b2, far1, far3, swapped = lax.optimization_barrier((e2, b2, far1, far3, swapped))
    b2 = b2.reshape(2, 4, slot, width)
    far1, far3 = [a.reshape(2, 1, slot, width) for a in (far1, far3)]
    others = swap_core(jnp.concatenate([b2[1], far1[1], far3[1]]))

    def in_order(whole0, part1, whole2, part3, rest1, rest3):
        part1, part3 = [[p[0], p[1], r[0], p[2]] for p, r in ((part1, rest1), (part3, rest3))]
        return [whole0, part1, whole2, part3]

    back = [
        in_order(back0[0], b1[0], b2[0], b3[0], far1[0], far3[0]),
        in_order(swapped[:4], swapped[4:7], others[:4], swapped[7:], others[4:5], others[5:]),
    ]

    def by_token(s):
        rows_of = jnp.stack([back[dc][t][s] for dc in range(2) for t in range(4)])
        return mm(pick_z[s], rows_of.reshape(-1, width))

    both = [
        (out0.astype(F32) + e2.astype(F32)).astype(BF).reshape(4, 2, slot, width),
        (e1.astype(F32) + e3.astype(F32)).astype(BF).reshape(4, 2, slot, width),
    ]
    both = [jnp.stack([a[t] for a in both]) for t in range(4)]
    m1, m3 = shift_y(both[1], -1), shift_y(both[3], -3)
    far = by_token(2).astype(BF)
    far_a, far_b = shift_z(far[:, :half], 1), shift_z(far[:, half:], -1)
    up_z, down_z, here = by_token(3), by_token(1), by_token(0)

    far_a, far_b, m1, m3, both_far = lax.optimization_barrier((far_a, far_b, m1, m3, both[2]))
    swapped = swap_core(jnp.stack([both[0][:, 1], m1[:, 1], m3[:, 1]]))
    a, b = slice(0, half), slice(half, width)

    def ends(part, up_rows, down_rows, far_rows):
        up_part, down_part = up_rows.astype(BF), down_rows.astype(BF)
        return shift_z(up_part, 1), shift_z(down_part, -1), shift_y(far_rows[:, :, :, part], -2)

    def finish(part, from_down, from_up, m2, swap):
        sib = [swap[0], swap[1], swap_core(m2[:, 1]), swap[2]]
        pieces = [both[0][:, 0], m1[:, 0], m3[:, 0]] + [swap[i] for i in range(3)]
        pieces = [p[..., part] for p in pieces]
        back = [pieces[0], pieces[1], m2[:, 0], pieces[2], pieces[3], pieces[4], sib[2], pieces[5]]
        back = jnp.stack(back).reshape(2 * flat, -1)
        mixed = sum(weights[:, k, None] * mm(each_y[k], back) for k in range(per_token)).astype(BF)
        grad = (here[:, part] + from_down.astype(F32) + from_up.astype(F32)).astype(BF)
        return from_behind(mixed, "section", 1), from_behind(grad, "section", -1)

    from_down, from_up, m2 = ends(a, up_z[:, a] + far_a.astype(F32), down_z[:, a], both_far)
    late_x, late_gate, _ = lax.optimization_barrier(((same, x1, x2, x3), gate_grad, far_a))

    def by_s(grads):
        return jnp.concatenate([grads[s, t] for s in range(4) for t in range(4)])

    late_x = jnp.concatenate(late_x)
    gate_total = mm_first(late_x, by_s(late_gate)).astype(BF)

    from_down, from_up, m2, swapped, up_b, down_b, far_rows = lax.optimization_barrier(
        (from_down, from_up, m2, swapped, up_z[:, b], down_z[:, b] + far_b.astype(F32), both_far)
    )
    next_a, prev_a = finish(a, from_down, from_up, m2, swapped)
    from_down, from_up, m2 = ends(b, up_b, down_b, far_rows)
    late_x, late_up, _ = lax.optimization_barrier((late_x, up_grad, swapped))
    up_total = mm_first(late_x, by_s(late_up)).astype(BF)

    next_a, prev_a, from_down, from_up, m2 = lax.optimization_barrier(
        (next_a, prev_a, from_down, from_up, m2)
    )
    next_b, prev_b = finish(b, from_down, from_up, m2, swapped)
    return (
        jnp.concatenate([next_a, next_b], axis=1)[None, None],
        jnp.concatenate([prev_a, prev_b], axis=1)[None, None],
        gate_total[None, None],
        up_total[None, None],
        down_total[None, None],
    )


def solution(mesh):
    return jax.shard_map(
        local,
        mesh=mesh,
        in_specs=(
            P("section", "dp", "expert", None),
            P("section", "dp", "expert", None),
            P("section", "dp", "expert", None),
            P("section", "dp", "expert", None),
            P("section", "expert", None, "dp"),
            P("section", "expert", None, "dp"),
            P("section", "expert", "dp", None),
        ),
        out_specs=(
            P("section", "dp", "expert", None),
            P("section", "dp", "expert", None),
            P("section", "expert", None, "dp"),
            P("section", "expert", None, "dp"),
            P("section", "expert", "dp", None),
        ),
        check_vma=False,
    )
```

```python
import jax
import jax.numpy as jnp
from jax import lax
from jax.experimental import pallas as pl
from jax.experimental.pallas import tpu as pltpu
from jax.sharding import PartitionSpec as P

GROUP = ("expert", "dp")
BF = jnp.bfloat16
F32 = jnp.float32


def place(y, z, c):
    return (((y * 2 + z % 2) * 2 + c) * 2) + z // 2


def shifted(x, dy, dz, dc):
    pairs = [
        (place(y, z, c), place((y + dy) % 4, (z + dz) % 4, c ^ dc))
        for y in range(4)
        for z in range(4)
        for c in range(2)
    ]
    return lax.ppermute(x, GROUP, pairs)


def shift_y(x, by):
    return x if by % 4 == 0 else shifted(x, by, 0, 0)


def shift_z(x, by):
    return x if by % 4 == 0 else shifted(x, 0, by, 0)


def swap_core(x):
    return shifted(x, 0, 0, 1)


def after(x, done):
    return lax.optimization_barrier((x, done))[0]


def from_behind(x, axis, by):
    count = lax.axis_size(axis)
    pairs = [(i, i + by) for i in range(count) if 0 <= i + by < count]
    return lax.ppermute(x, axis, pairs)


def slot_codes(ids, experts, slot_rows):
    rows = ids.shape[-2]
    onehot = (ids[..., None] == jnp.arange(experts, dtype=F32)).astype(F32)
    named = jnp.sum(onehot, axis=-2).astype(BF)
    before = jnp.tri(rows, k=-1, dtype=BF)
    earlier = jnp.einsum("ij,...je->...ie", before, named, preferred_element_type=F32)
    position = jnp.sum(onehot * earlier[..., None, :], axis=-1)
    return (ids * slot_rows + position).astype(jnp.int32)


def chosen(codes, weights, targets):
    hits = [codes[..., k, None] == targets for k in range(codes.shape[-1])]
    weight = sum(jnp.sum(jnp.where(h, weights[..., k, None], 0.0), axis=-2) for k, h in enumerate(hits))
    return [h.astype(BF) for h in hits], hits[0].astype(BF) + hits[1].astype(BF), weight


def in_three(w):
    high = lax.reduce_precision(w, 8, 7)
    middle = lax.reduce_precision(w - high, 8, 7)
    return high, middle, w - high - middle


def mm(a, b):
    return jnp.dot(a, b, preferred_element_type=F32)


def mm_last(a, b):
    return lax.dot_general(a, b, (((1,), (1,)), ((), ())), preferred_element_type=F32)


def mm_first(a, b):
    return lax.dot_general(a, b, (((0,), (0,)), ((), ())), preferred_element_type=F32)


def kernel_call(body, grid, in_specs, out_specs, out_shape, scratch=()):
    return pl.pallas_call(
        body,
        grid=(grid,),
        in_specs=in_specs,
        out_specs=out_specs,
        out_shape=out_shape,
        scratch_shapes=scratch,
        compiler_params=pltpu.CompilerParams(vmem_limit_bytes=40 * 1024 * 1024),
        cost_estimate=pl.CostEstimate(flops=1, bytes_accessed=1, transcendentals=0),
    )


def whole(x):
    return pl.BlockSpec(x.shape, lambda i: (0, 0))


def columns(rows, n):
    return pl.BlockSpec((rows, n), lambda i: (0, i))


def rows_block(n, width):
    return pl.BlockSpec((n, width), lambda i: (i, 0))


def forward(pieces, gate_matrix, up_matrix):
    count, rows = len(pieces), pieces[0].shape[0]
    depth, units = gate_matrix.shape
    n = units // 2

    def body(*refs):
        gate, up, outs = refs[count], refs[count + 1], refs[count + 2 :]
        for i in range(count):
            x = refs[i][...]
            g, u = mm(x, gate[...]), mm(x, up[...])
            outs[3 * i][...] = g
            outs[3 * i + 1][...] = u
            outs[3 * i + 2][...] = (g * jax.nn.sigmoid(g) * u).astype(BF)

    shapes = [jax.ShapeDtypeStruct((rows, units), t) for t in (F32, F32, BF)] * count
    outs = kernel_call(
        body,
        2,
        [whole(x) for x in pieces] + [columns(depth, n)] * 2,
        [columns(rows, n)] * (3 * count),
        shapes,
    )(*pieces, gate_matrix, up_matrix)
    return [outs[3 * i : 3 * i + 3] for i in range(count)]


def outputs(hidden, down_matrix):
    count, rows = len(hidden), hidden[0].shape[0]
    units, width = down_matrix.shape
    n = width // 7

    def body(*refs):
        for i in range(count):
            refs[count + 1 + i][...] = mm(refs[i][...], refs[count][...]).astype(BF)

    return kernel_call(
        body,
        7,
        [whole(h) for h in hidden] + [columns(units, n)],
        [columns(rows, n)] * count,
        [jax.ShapeDtypeStruct((rows, width), BF)] * count,
    )(*hidden, down_matrix)


def hidden_grads(pieces, down_matrix):
    count, rows = len(pieces), pieces[0].shape[0]
    units, width = down_matrix.shape
    n = units // 2

    def body(*refs):
        for i in range(count):
            refs[count + 1 + i][...] = mm_last(refs[i][...], refs[count][...])

    return kernel_call(
        body,
        2,
        [whole(g) for g in pieces] + [rows_block(n, width)],
        [columns(rows, n)] * count,
        [jax.ShapeDtypeStruct((rows, units), F32)] * count,
    )(*pieces, down_matrix)


def backward(groups, slot, gate_pre, up_pre, hidden_grad, gate_matrix, up_matrix):
    used_s = sorted({s for _, those in groups for s in those})
    pairs = sorted((s, t) for t, those in groups for s in those)
    rows, units = gate_pre[used_s[0]].shape
    width = gate_matrix.shape[0]
    n = width // 7
    counts = [2 * len(those) * slot for _, those in groups]
    starts = [sum(counts[:i]) for i in range(len(groups))]
    total = sum(counts)
    many, those_s = len(groups), len(used_s)

    def body(*refs):
        gates = dict(zip(used_s, refs[:those_s]))
        ups = dict(zip(used_s, refs[those_s : 2 * those_s]))
        refs = refs[2 * those_s :]
        grads, (gate, up), refs = refs[:many], refs[many : many + 2], refs[many + 2 :]
        backs, (gate_out, up_out, gate_rows, up_rows) = refs[:many], refs[many:]

        @pl.when(pl.program_id(0) == 0)
        def _():
            for i, (t, those) in enumerate(groups):
                terms = {}
                for d in range(2):
                    for s in those:
                        here = pl.ds((t * 2 + d) * slot, slot)
                        g, u = gates[s][here, :], ups[s][here, :]
                        h = grads[i][pl.ds((d * 4 + s) * slot, slot), :]
                        sig = jax.nn.sigmoid(g)
                        terms[d, s] = (h * u * sig * (1.0 + g * (1.0 - sig)), h * g * sig)
                order = [terms[d, s] for d in range(2) for s in those]
                for which, by_t, by_s in ((0, gate_rows, gate_out), (1, up_rows, up_out)):
                    for k in range(0, len(order), 2):
                        pair = jnp.concatenate([order[k][which], order[k + 1][which]], axis=0)
                        by_t[pl.ds(starts[i] + k * slot, 2 * slot), :] = pair.astype(BF)
                    for s in those:
                        pair = jnp.concatenate([terms[0, s][which], terms[1, s][which]], axis=0)
                        by_s[pl.ds(pairs.index((s, t)) * 2 * slot, 2 * slot), :] = pair.astype(BF)

        back = mm_last(gate_rows[...], gate[...]) + mm_last(up_rows[...], up[...])
        for i in range(many):
            backs[i][...] = back[starts[i] : starts[i] + counts[i]].astype(BF)

    both = jax.ShapeDtypeStruct((total, units), BF)
    operands = [gate_pre[s] for s in used_s] + [up_pre[s] for s in used_s]
    operands += [hidden_grad[t] for t, _ in groups]
    outs = kernel_call(
        body,
        7,
        [whole(a) for a in operands] + [rows_block(n, units)] * 2,
        [columns(count, n) for count in counts] + [whole(both)] * 2,
        [jax.ShapeDtypeStruct((count, width), BF) for count in counts] + [both] * 2,
        [pltpu.VMEM(both.shape, BF)] * 2,
    )(*operands, gate_matrix, up_matrix)
    grads = [
        {pair: a[k * 2 * slot : (k + 1) * 2 * slot] for k, pair in enumerate(pairs)} for a in outs[many:]
    ]
    return outs[:many], grads[0], grads[1]


def local(tokens, grad_out, expert_ids, route_weight, w_gate, w_up, w_down):
    inputs = tokens[0, 0]
    upstream = grad_out[0, 0]
    weights = route_weight[0, 0]
    gate_matrix, up_matrix, down_matrix = w_gate[0, 0], w_up[0, 0], w_down[0, 0]
    experts = lax.axis_size("expert")
    rows, per_token = weights.shape
    width = inputs.shape[1]
    split = rows // 2
    slot = 3 * rows * per_token // (2 * experts)
    flat = 8 * slot
    me = lax.axis_index("expert")
    y, zl, c = me // 4, (me // 2) % 2, me % 2

    ids = expert_ids[0, 0].astype(F32)
    fields = [ids] + [jnp.stack([a[:, k] for a in in_three(weights)], axis=1) for k in range(per_token)]
    fields = jnp.concatenate(fields, axis=1).astype(BF)
    codes = slot_codes(ids, experts, slot)
    step = jnp.arange(4, dtype=jnp.int32)
    two = jnp.arange(2, dtype=jnp.int32)
    slots = jnp.arange(slot, dtype=jnp.int32)
    dest_y = ((y + step) % 4) * 4
    targets_z = (
        (dest_y[None, :, None] + zl * 2 + (c ^ two)[:, None, None]) * slot + slots
    ).reshape(-1)
    targets_y = (
        (
            dest_y[None, :, None, None]
            + (zl ^ two)[None, None, :, None] * 2
            + (c ^ two)[:, None, None, None]
        )
        * slot
        + slots
    ).reshape(-1)
    each_y, pick_y, _ = chosen(codes, weights, targets_y)
    own, sib = [
        mm_first(pick_y[:, dc * flat : (dc + 1) * flat], inputs).astype(BF).reshape(4, 2, slot, width)
        for dc in range(2)
    ]
    message = jnp.concatenate(
        [after(upstream, sib), jnp.pad(fields.T, ((0, 0), (0, width - rows)))], axis=0
    )
    near1, near3 = shift_z(message, 1), shift_z(message, 3)
    sib = swap_core(sib)
    along_y = [jnp.stack([own[t], sib[t]]) for t in range(4)]
    y1, y3 = shift_y(along_y[1], 1), shift_y(along_y[3], 3)

    near1, near3, y1, y3, far_y = lax.optimization_barrier((near1, near3, y1, y3, along_y[2]))
    y2 = shift_y(far_y, 2)
    far_a, far_b = shift_z(near1[:split], 1), shift_z(near3[split:], 3)
    ring_tables = [fields, near1[rows:, :rows].T, far_b[rows - split :, :rows].T, near3[rows:, :rows].T]

    def picks(table):
        table = table.astype(F32)
        parts = [table[:, per_token + 3 * k : per_token + 3 * k + 3] for k in range(per_token)]
        weigh = jnp.stack([p[:, 0] + p[:, 1] + p[:, 2] for p in parts], axis=-1)
        return chosen(slot_codes(table[:, :per_token], experts, slot), weigh, targets_z)[1:]

    pick_z, slot_weight_z = zip(*[picks(a) for a in ring_tables])
    far_a, far_b, near1, near3, late_upstream = lax.optimization_barrier(
        (far_a, far_b, near1, near3, upstream)
    )
    far = jnp.concatenate([far_a, far_b[: rows - split]])
    sel = [
        (slot_weight_z[s][:, None] * mm_first(pick_z[s], block)).astype(BF).reshape(2, 4, slot, width)
        for s, block in enumerate((late_upstream, near1[:rows], far, near3[:rows]))
    ]
    cross = [jnp.stack([a[1, t] for t in those for a in sel]) for those in ((1, 3), (0, 2))]

    sel, cross, y1, y2, y3 = lax.optimization_barrier((sel, cross, y1, y2, y3))
    by_y = [along_y[0], y1, y2, y3]
    same, other = [jnp.stack([a[:, dl] for a in by_y]).reshape(flat, width) for dl in range(2)]
    x1, x3 = shift_z(other, 1), shift_z(other, 3)
    odd, even = swap_core(cross[0]), swap_core(cross[1])
    sib = [even[:4], odd[:4], even[4:], odd[4:]]
    out_y = [
        jnp.concatenate([jnp.stack([sel[s][0, t] for s in range(4)]), sib[t]]).reshape(flat, width)
        for t in range(4)
    ]
    g1, g3 = shift_y(out_y[1], 1), shift_y(out_y[3], 3)

    x1, x3, g1, g3, same_far, out_far = lax.optimization_barrier((x1, x3, g1, g3, same, out_y[2]))
    x2, g2 = shift_z(same_far, 2), shift_y(out_far, 2)
    ahead = forward([x1, x3, same_far], gate_matrix, up_matrix)
    out1, out3 = outputs([ahead[0][2], ahead[1][2]], down_matrix)
    grad1, grad3, grad0 = hidden_grads([g1, g3, out_y[0]], down_matrix)
    gate_pre, up_pre, hidden = [{0: ahead[2][i], 1: ahead[0][i], 3: ahead[1][i]} for i in range(3)]
    early = ((1, (0, 1, 3)), (3, (0, 1, 3)))
    (back1, back3), gate_grad, up_grad = backward(
        early, slot, gate_pre, up_pre, {1: grad1, 3: grad3}, gate_matrix, up_matrix
    )

    x2, g2, out1, out3, back1, back3 = lax.optimization_barrier((x2, g2, out1, out3, back1, back3))
    e1, e3 = shift_z(out1, -1), shift_z(out3, -3)
    b1, b3 = shift_y(back1, -1), shift_y(back3, -3)
    ((gate_pre[2], up_pre[2], hidden[2]),) = forward([x2], gate_matrix, up_matrix)
    (grad2,) = hidden_grads([g2], down_matrix)
    out2, out0 = outputs([hidden[2], hidden[0]], down_matrix)
    rest = ((0, (0, 1, 2, 3)), (2, (0, 1, 2, 3)), (1, (2,)), (3, (2,)))
    (back0, back2, back1, back3), more_gate, more_up = backward(
        rest,
        slot,
        gate_pre,
        up_pre,
        {0: grad0, 1: grad1, 2: grad2, 3: grad3},
        gate_matrix,
        up_matrix,
    )
    gate_grad, up_grad = {**gate_grad, **more_gate}, {**up_grad, **more_up}

    e1, e3, b1, b3, out0, out2, back0, back1, back2, back3 = lax.optimization_barrier(
        (e1, e3, b1, b3, out0, out2, back0, back1, back2, back3)
    )
    e2, b2 = shift_z(out2, -2), shift_y(back2, -2)
    far1, far3 = shift_y(back1, -1), shift_y(back3, -3)
    back0 = back0.reshape(2, 4, slot, width)
    b1, b3 = [a.reshape(2, 3, slot, width) for a in (b1, b3)]
    swapped = swap_core(jnp.concatenate([back0[1], b1[1], b3[1]]))
    late_g, late_hidden, _ = lax.optimization_barrier(((out_y[0], g1, g2, g3), hidden, e1))
    late_hidden = jnp.stack([late_hidden[s].reshape(4, 2, slot, -1) for s in range(4)], axis=2)
    down_total = mm_first(late_hidden.reshape(4 * flat, -1), jnp.concatenate(late_g)).astype(BF)

    e2, b2, far1, far3, swapped = lax.optimization_barrier((e2, b2, far1, far3, swapped))
    b2 = b2.reshape(2, 4, slot, width)
    far1, far3 = [a.reshape(2, 1, slot, width) for a in (far1, far3)]
    others = swap_core(jnp.concatenate([b2[1], far1[1], far3[1]]))

    def in_order(whole0, part1, whole2, part3, rest1, rest3):
        part1, part3 = [[p[0], p[1], r[0], p[2]] for p, r in ((part1, rest1), (part3, rest3))]
        return [whole0, part1, whole2, part3]

    back = [
        in_order(back0[0], b1[0], b2[0], b3[0], far1[0], far3[0]),
        in_order(swapped[:4], swapped[4:7], others[:4], swapped[7:], others[4:5], others[5:]),
    ]

    def by_token(s):
        rows_of = jnp.stack([back[dc][t][s] for dc in range(2) for t in range(4)])
        return mm(pick_z[s], rows_of.reshape(-1, width))

    both = [
        (out0.astype(F32) + e2.astype(F32)).astype(BF).reshape(4, 2, slot, width),
        (e1.astype(F32) + e3.astype(F32)).astype(BF).reshape(4, 2, slot, width),
    ]
    both = [jnp.stack([a[t] for a in both]) for t in range(4)]
    m1, m3 = shift_y(both[1], -1), shift_y(both[3], -3)
    far = by_token(2).astype(BF)
    far_a, far_b = shift_z(far[:split], 1), shift_z(far[split:], -1)
    up_z, down_z, here = by_token(3), by_token(1), by_token(0)

    far_a, far_b, m1, m3, both_far = lax.optimization_barrier((far_a, far_b, m1, m3, both[2]))
    up_z = jnp.concatenate([up_z[:split] + far_a.astype(F32), up_z[split:]]).astype(BF)
    down_z = jnp.concatenate([down_z[:split], down_z[split:] + far_b.astype(F32)]).astype(BF)
    from_down, from_up = shift_z(up_z, 1), shift_z(down_z, -1)
    m2 = shift_y(both_far, -2)
    swapped = swap_core(jnp.stack([both[0][:, 1], m1[:, 1], m3[:, 1]]))
    late_x, late_gate, _ = lax.optimization_barrier(((same, x1, x2, x3), gate_grad, far_a))

    def by_s(grads):
        return jnp.concatenate([grads[s, t] for s in range(4) for t in range(4)])

    late_x = jnp.concatenate(late_x)
    gate_total = mm_first(late_x, by_s(late_gate)).astype(BF)

    sib = [swapped[0], swapped[1], swap_core(m2[:, 1]), swapped[2]]
    back = jnp.stack([both[0][:, 0], m1[:, 0], m2[:, 0], m3[:, 0]] + sib).reshape(-1, width)
    mixed = sum(weights[:, k, None] * mm(each_y[k], back) for k in range(per_token)).astype(BF)
    next_input = from_behind(mixed, "section", 1)
    input_grad = (here + from_down.astype(F32) + from_up.astype(F32)).astype(BF)
    prev_grad = from_behind(input_grad, "section", -1)
    late_x, late_up, _ = lax.optimization_barrier((late_x, up_grad, m2))
    up_total = mm_first(late_x, by_s(late_up)).astype(BF)
    return (
        next_input[None, None],
        prev_grad[None, None],
        gate_total[None, None],
        up_total[None, None],
        down_total[None, None],
    )


def solution(mesh):
    return jax.shard_map(
        local,
        mesh=mesh,
        in_specs=(
            P("section", "dp", "expert", None),
            P("section", "dp", "expert", None),
            P("section", "dp", "expert", None),
            P("section", "dp", "expert", None),
            P("section", "expert", None, "dp"),
            P("section", "expert", None, "dp"),
            P("section", "expert", "dp", None),
        ),
        out_specs=(
            P("section", "dp", "expert", None),
            P("section", "dp", "expert", None),
            P("section", "expert", None, "dp"),
            P("section", "expert", None, "dp"),
            P("section", "expert", "dp", None),
        ),
        check_vma=False,
    )
```

```python
import jax
import jax.numpy as jnp
from jax import lax
from jax.experimental import pallas as pl
from jax.experimental.pallas import tpu as pltpu
from jax.sharding import PartitionSpec as P

GROUP = ("expert", "dp")
BF = jnp.bfloat16
F32 = jnp.float32


def place(y, z, c):
    return (((y * 2 + z % 2) * 2 + c) * 2) + z // 2


def shifted(x, dy, dz, dc):
    pairs = [
        (place(y, z, c), place((y + dy) % 4, (z + dz) % 4, c ^ dc))
        for y in range(4)
        for z in range(4)
        for c in range(2)
    ]
    return lax.ppermute(x, GROUP, pairs)


def shift_y(x, by):
    return x if by % 4 == 0 else shifted(x, by, 0, 0)


def shift_z(x, by):
    return x if by % 4 == 0 else shifted(x, 0, by, 0)


def swap_core(x):
    return shifted(x, 0, 0, 1)


def after(x, done):
    return lax.optimization_barrier((x, done))[0]


def from_behind(x, axis, by):
    count = lax.axis_size(axis)
    pairs = [(i, i + by) for i in range(count) if 0 <= i + by < count]
    return lax.ppermute(x, axis, pairs)


def slot_codes(ids, experts, slot_rows):
    rows = ids.shape[-2]
    onehot = (ids[..., None] == jnp.arange(experts, dtype=F32)).astype(F32)
    named = jnp.sum(onehot, axis=-2).astype(BF)
    before = jnp.tri(rows, k=-1, dtype=BF)
    earlier = jnp.einsum("ij,...je->...ie", before, named, preferred_element_type=F32)
    position = jnp.sum(onehot * earlier[..., None, :], axis=-1)
    return (ids * slot_rows + position).astype(jnp.int32)


def chosen(codes, weights, targets):
    hits = [codes[..., k, None] == targets for k in range(codes.shape[-1])]
    weight = sum(jnp.sum(jnp.where(h, weights[..., k, None], 0.0), axis=-2) for k, h in enumerate(hits))
    return [h.astype(BF) for h in hits], hits[0].astype(BF) + hits[1].astype(BF), weight


def in_three(w):
    high = lax.reduce_precision(w, 8, 7)
    middle = lax.reduce_precision(w - high, 8, 7)
    return high, middle, w - high - middle


def mm(a, b):
    return jnp.dot(a, b, preferred_element_type=F32)


def mm_last(a, b):
    return lax.dot_general(a, b, (((1,), (1,)), ((), ())), preferred_element_type=F32)


def mm_first(a, b):
    return lax.dot_general(a, b, (((0,), (0,)), ((), ())), preferred_element_type=F32)


def kernel_call(body, grid, in_specs, out_specs, out_shape, scratch=()):
    return pl.pallas_call(
        body,
        grid=(grid,),
        in_specs=in_specs,
        out_specs=out_specs,
        out_shape=out_shape,
        scratch_shapes=scratch,
        compiler_params=pltpu.CompilerParams(vmem_limit_bytes=40 * 1024 * 1024),
        cost_estimate=pl.CostEstimate(flops=1, bytes_accessed=1, transcendentals=0),
    )


def whole(x):
    return pl.BlockSpec(x.shape, lambda i: (0, 0))


def columns(rows, n):
    return pl.BlockSpec((rows, n), lambda i: (0, i))


def rows_block(n, width):
    return pl.BlockSpec((n, width), lambda i: (i, 0))


def forward(pieces, gate_matrix, up_matrix):
    count, rows = len(pieces), pieces[0].shape[0]
    depth, units = gate_matrix.shape
    n = units // 2

    def body(*refs):
        gate, up, outs = refs[count], refs[count + 1], refs[count + 2 :]
        for i in range(count):
            x = refs[i][...]
            g, u = mm(x, gate[...]), mm(x, up[...])
            outs[3 * i][...] = g
            outs[3 * i + 1][...] = u
            outs[3 * i + 2][...] = (g * jax.nn.sigmoid(g) * u).astype(BF)

    shapes = [jax.ShapeDtypeStruct((rows, units), t) for t in (F32, F32, BF)] * count
    outs = kernel_call(
        body,
        2,
        [whole(x) for x in pieces] + [columns(depth, n)] * 2,
        [columns(rows, n)] * (3 * count),
        shapes,
    )(*pieces, gate_matrix, up_matrix)
    return [outs[3 * i : 3 * i + 3] for i in range(count)]


def outputs(hidden, down_matrix):
    count, rows = len(hidden), hidden[0].shape[0]
    units, width = down_matrix.shape
    n = width // 7

    def body(*refs):
        for i in range(count):
            refs[count + 1 + i][...] = mm(refs[i][...], refs[count][...]).astype(BF)

    return kernel_call(
        body,
        7,
        [whole(h) for h in hidden] + [columns(units, n)],
        [columns(rows, n)] * count,
        [jax.ShapeDtypeStruct((rows, width), BF)] * count,
    )(*hidden, down_matrix)


def hidden_grads(pieces, down_matrix):
    count, rows = len(pieces), pieces[0].shape[0]
    units, width = down_matrix.shape
    n = units // 2

    def body(*refs):
        for i in range(count):
            refs[count + 1 + i][...] = mm_last(refs[i][...], refs[count][...])

    return kernel_call(
        body,
        2,
        [whole(g) for g in pieces] + [rows_block(n, width)],
        [columns(rows, n)] * count,
        [jax.ShapeDtypeStruct((rows, units), F32)] * count,
    )(*pieces, down_matrix)


def backward(groups, slot, gate_pre, up_pre, hidden_grad, gate_matrix, up_matrix):
    used_s = sorted({s for _, those in groups for s in those})
    pairs = sorted((s, t) for t, those in groups for s in those)
    rows, units = gate_pre[used_s[0]].shape
    width = gate_matrix.shape[0]
    n = width // 7
    counts = [2 * len(those) * slot for _, those in groups]
    starts = [sum(counts[:i]) for i in range(len(groups))]
    total = sum(counts)
    many, those_s = len(groups), len(used_s)

    def body(*refs):
        gates = dict(zip(used_s, refs[:those_s]))
        ups = dict(zip(used_s, refs[those_s : 2 * those_s]))
        refs = refs[2 * those_s :]
        grads, (gate, up), refs = refs[:many], refs[many : many + 2], refs[many + 2 :]
        backs, (gate_out, up_out, gate_rows, up_rows) = refs[:many], refs[many:]

        @pl.when(pl.program_id(0) == 0)
        def _():
            for i, (t, those) in enumerate(groups):
                terms = {}
                for d in range(2):
                    for s in those:
                        here = pl.ds((t * 2 + d) * slot, slot)
                        g, u = gates[s][here, :], ups[s][here, :]
                        h = grads[i][pl.ds((d * 4 + s) * slot, slot), :]
                        sig = jax.nn.sigmoid(g)
                        terms[d, s] = (h * u * sig * (1.0 + g * (1.0 - sig)), h * g * sig)
                order = [terms[d, s] for d in range(2) for s in those]
                for which, by_t, by_s in ((0, gate_rows, gate_out), (1, up_rows, up_out)):
                    for k in range(0, len(order), 2):
                        pair = jnp.concatenate([order[k][which], order[k + 1][which]], axis=0)
                        by_t[pl.ds(starts[i] + k * slot, 2 * slot), :] = pair.astype(BF)
                    for s in those:
                        pair = jnp.concatenate([terms[0, s][which], terms[1, s][which]], axis=0)
                        by_s[pl.ds(pairs.index((s, t)) * 2 * slot, 2 * slot), :] = pair.astype(BF)

        back = mm_last(gate_rows[...], gate[...]) + mm_last(up_rows[...], up[...])
        for i in range(many):
            backs[i][...] = back[starts[i] : starts[i] + counts[i]].astype(BF)

    both = jax.ShapeDtypeStruct((total, units), BF)
    operands = [gate_pre[s] for s in used_s] + [up_pre[s] for s in used_s]
    operands += [hidden_grad[t] for t, _ in groups]
    outs = kernel_call(
        body,
        7,
        [whole(a) for a in operands] + [rows_block(n, units)] * 2,
        [columns(count, n) for count in counts] + [whole(both)] * 2,
        [jax.ShapeDtypeStruct((count, width), BF) for count in counts] + [both] * 2,
        [pltpu.VMEM(both.shape, BF)] * 2,
    )(*operands, gate_matrix, up_matrix)
    grads = [
        {pair: a[k * 2 * slot : (k + 1) * 2 * slot] for k, pair in enumerate(pairs)} for a in outs[many:]
    ]
    return outs[:many], grads[0], grads[1]


def weight_grads(lefts, rights, by_rows):
    count, many = len(lefts), len(rights)
    rows, wide = lefts[0].shape
    units = rights[0][0].shape[1]

    def body(*refs):
        for k in range(many):
            terms = [
                mm_first(refs[i][...], refs[count * (k + 1) + i][...]) for i in range(count)
            ]
            refs[count * (many + 1) + k][...] = sum(terms[1:], terms[0]).astype(BF)

    if by_rows:
        left, right = columns(rows, wide // 7), whole(rights[0][0])
        out = rows_block(wide // 7, units)
    else:
        left, right = whole(lefts[0]), columns(rows, units // 7)
        out = columns(wide, units // 7)
    return kernel_call(
        body,
        7,
        [left] * count + [right] * (count * many),
        [out] * many,
        [jax.ShapeDtypeStruct((wide, units), BF)] * many,
    )(*lefts, *[r for those in rights for r in those])


def local(tokens, grad_out, expert_ids, route_weight, w_gate, w_up, w_down):
    inputs = tokens[0, 0]
    upstream = grad_out[0, 0]
    weights = route_weight[0, 0]
    gate_matrix, up_matrix, down_matrix = w_gate[0, 0], w_up[0, 0], w_down[0, 0]
    experts = lax.axis_size("expert")
    rows, per_token = weights.shape
    width = inputs.shape[1]
    split = rows // 2
    slot = 3 * rows * per_token // (2 * experts)
    flat = 8 * slot
    me = lax.axis_index("expert")
    y, zl, c = me // 4, (me // 2) % 2, me % 2

    ids = expert_ids[0, 0].astype(F32)
    fields = [ids] + [jnp.stack([a[:, k] for a in in_three(weights)], axis=1) for k in range(per_token)]
    fields = jnp.concatenate(fields, axis=1).astype(BF)
    codes = slot_codes(ids, experts, slot)
    step = jnp.arange(4, dtype=jnp.int32)
    two = jnp.arange(2, dtype=jnp.int32)
    slots = jnp.arange(slot, dtype=jnp.int32)
    dest_y = ((y + step) % 4) * 4
    targets_z = (
        (dest_y[None, :, None] + zl * 2 + (c ^ two)[:, None, None]) * slot + slots
    ).reshape(-1)
    targets_y = (
        (
            dest_y[None, :, None, None]
            + (zl ^ two)[None, None, :, None] * 2
            + (c ^ two)[:, None, None, None]
        )
        * slot
        + slots
    ).reshape(-1)
    each_y, pick_y, _ = chosen(codes, weights, targets_y)
    own, sib = [
        mm_first(pick_y[:, dc * flat : (dc + 1) * flat], inputs).astype(BF).reshape(4, 2, slot, width)
        for dc in range(2)
    ]
    message = jnp.concatenate(
        [after(upstream, sib), jnp.pad(fields.T, ((0, 0), (0, width - rows)))], axis=0
    )
    near1, near3 = shift_z(message, 1), shift_z(message, 3)
    sib = swap_core(sib)
    along_y = [jnp.stack([own[t], sib[t]]) for t in range(4)]
    y1, y3 = shift_y(along_y[1], 1), shift_y(along_y[3], 3)

    near1, near3, y1, y3, far_y = lax.optimization_barrier((near1, near3, y1, y3, along_y[2]))
    y2 = shift_y(far_y, 2)
    far_a, far_b = shift_z(near1[:split], 1), shift_z(near3[split:], 3)
    ring_tables = [fields, near1[rows:, :rows].T, far_b[rows - split :, :rows].T, near3[rows:, :rows].T]

    def picks(table):
        table = table.astype(F32)
        parts = [table[:, per_token + 3 * k : per_token + 3 * k + 3] for k in range(per_token)]
        weigh = jnp.stack([p[:, 0] + p[:, 1] + p[:, 2] for p in parts], axis=-1)
        return chosen(slot_codes(table[:, :per_token], experts, slot), weigh, targets_z)[1:]

    pick_z, slot_weight_z = zip(*[picks(a) for a in ring_tables])

    def select(s, block):
        picked = slot_weight_z[s][:, None] * mm_first(pick_z[s], block)
        return picked.astype(BF).reshape(2, 4, slot, width)

    sel = {0: select(0, upstream), 1: select(1, near1[:rows]), 3: select(3, near3[:rows])}
    y1, y2, y3, sel = lax.optimization_barrier((y1, y2, y3, sel))
    by_y = [along_y[0], y1, y2, y3]
    same, other = [jnp.stack([a[:, dl] for a in by_y]).reshape(flat, width) for dl in range(2)]
    far_a, far_b, sel, same, other = lax.optimization_barrier((far_a, far_b, sel, same, other))
    sel[2] = select(2, jnp.concatenate([far_a, far_b[: rows - split]]))

    cross = [jnp.stack([sel[s][1, t] for t in those for s in range(4)]) for those in ((1, 3), (0, 2))]
    odd = swap_core(cross[0])
    odd, other, cross_even = lax.optimization_barrier((odd, other, cross[1]))
    even = swap_core(cross_even)
    x1, x3 = shift_z(other, 1), shift_z(other, 3)
    sib = [even[:4], odd[:4], even[4:], odd[4:]]
    out_y = [
        jnp.concatenate([jnp.stack([sel[s][0, t] for s in range(4)]), sib[t]]).reshape(flat, width)
        for t in range(4)
    ]
    g1, g3 = shift_y(out_y[1], 1), shift_y(out_y[3], 3)

    x1, x3, g1, g3, same_far, out_far = lax.optimization_barrier((x1, x3, g1, g3, same, out_y[2]))
    x2, g2 = shift_z(same_far, 2), shift_y(out_far, 2)
    ahead = forward([x1, x3, same_far], gate_matrix, up_matrix)
    out1, out3 = outputs([ahead[0][2], ahead[1][2]], down_matrix)
    grad1, grad3, grad0 = hidden_grads([g1, g3, out_y[0]], down_matrix)
    gate_pre, up_pre, hidden = [{0: ahead[2][i], 1: ahead[0][i], 3: ahead[1][i]} for i in range(3)]
    early = ((1, (0, 1, 3)), (3, (0, 1, 3)))
    (back1, back3), gate_grad, up_grad = backward(
        early, slot, gate_pre, up_pre, {1: grad1, 3: grad3}, gate_matrix, up_matrix
    )

    x2, g2, out1, out3, back1, back3 = lax.optimization_barrier((x2, g2, out1, out3, back1, back3))
    e1, e3 = shift_z(out1, -1), shift_z(out3, -3)
    b1, b3 = shift_y(back1, -1), shift_y(back3, -3)
    ((gate_pre[2], up_pre[2], hidden[2]),) = forward([x2], gate_matrix, up_matrix)
    (grad2,) = hidden_grads([g2], down_matrix)
    out2, out0 = outputs([hidden[2], hidden[0]], down_matrix)
    rest = ((0, (0, 1, 2, 3)), (2, (0, 1, 2, 3)), (1, (2,)), (3, (2,)))
    (back0, back2, back1, back3), more_gate, more_up = backward(
        rest,
        slot,
        gate_pre,
        up_pre,
        {0: grad0, 1: grad1, 2: grad2, 3: grad3},
        gate_matrix,
        up_matrix,
    )
    gate_grad, up_grad = {**gate_grad, **more_gate}, {**up_grad, **more_up}

    e1, e3, b1, b3, out0, out2, back0, back1, back2, back3 = lax.optimization_barrier(
        (e1, e3, b1, b3, out0, out2, back0, back1, back2, back3)
    )
    e2, b2 = shift_z(out2, -2), shift_y(back2, -2)
    far1, far3 = shift_y(back1, -1), shift_y(back3, -3)
    back0 = back0.reshape(2, 4, slot, width)
    b1, b3 = [a.reshape(2, 3, slot, width) for a in (b1, b3)]
    swapped = swap_core(jnp.concatenate([back0[1], b1[1], b3[1]]))
    late_g, late_hidden, _ = lax.optimization_barrier(((out_y[0], g1, g2, g3), hidden, e1))
    late_hidden = [late_hidden[s].reshape(4, 2, slot, -1) for s in range(4)]
    late_hidden = [jnp.stack([h[t] for h in late_hidden], axis=1).reshape(flat, -1) for t in range(4)]
    (down_total,) = weight_grads(late_hidden, [late_g], False)

    e2, b2, far1, far3, swapped, down_total = lax.optimization_barrier(
        (e2, b2, far1, far3, swapped, down_total)
    )
    b2 = b2.reshape(2, 4, slot, width)
    far1, far3 = [a.reshape(2, 1, slot, width) for a in (far1, far3)]
    others = swap_core(jnp.concatenate([b2[1], far1[1], far3[1]]))

    def in_order(whole0, part1, whole2, part3, rest1, rest3):
        part1, part3 = [[p[0], p[1], r[0], p[2]] for p, r in ((part1, rest1), (part3, rest3))]
        return [whole0, part1, whole2, part3]

    back = [
        in_order(back0[0], b1[0], b2[0], b3[0], far1[0], far3[0]),
        in_order(swapped[:4], swapped[4:7], others[:4], swapped[7:], others[4:5], others[5:]),
    ]

    def by_token(s):
        rows_of = jnp.stack([back[dc][t][s] for dc in range(2) for t in range(4)])
        return mm(pick_z[s], rows_of.reshape(-1, width))

    both = [
        (out0.astype(F32) + e2.astype(F32)).astype(BF).reshape(4, 2, slot, width),
        (e1.astype(F32) + e3.astype(F32)).astype(BF).reshape(4, 2, slot, width),
    ]
    both = [jnp.stack([a[t] for a in both]) for t in range(4)]
    m1, m3 = shift_y(both[1], -1), shift_y(both[3], -3)
    far = by_token(2).astype(BF)
    far_a, far_b = shift_z(far[:split], 1), shift_z(far[split:], -1)
    up_z, down_z, here = by_token(3), by_token(1), by_token(0)

    far_a, far_b, m1, m3, both_far = lax.optimization_barrier((far_a, far_b, m1, m3, both[2]))
    up_z = jnp.concatenate([up_z[:split] + far_a.astype(F32), up_z[split:]]).astype(BF)
    down_z = jnp.concatenate([down_z[:split], down_z[split:] + far_b.astype(F32)]).astype(BF)
    from_down, from_up = shift_z(up_z, 1), shift_z(down_z, -1)
    m2 = shift_y(both_far, -2)
    swapped = swap_core(jnp.stack([both[0][:, 1], m1[:, 1], m3[:, 1]]))
    late_x, late_gate, late_up, _ = lax.optimization_barrier(
        ((same, x1, x2, x3), gate_grad, up_grad, far_a)
    )

    def by_s(grads):
        return [jnp.concatenate([grads[s, t] for t in range(4)]) for s in range(4)]

    gate_total, up_total = weight_grads(late_x, [by_s(late_gate), by_s(late_up)], True)
    m2, from_down, from_up, gate_total, up_total = lax.optimization_barrier(
        (m2, from_down, from_up, gate_total, up_total)
    )

    sib = [swapped[0], swapped[1], swap_core(m2[:, 1]), swapped[2]]
    back = jnp.stack([both[0][:, 0], m1[:, 0], m2[:, 0], m3[:, 0]] + sib).reshape(-1, width)
    mixed = sum(weights[:, k, None] * mm(each_y[k], back) for k in range(per_token)).astype(BF)
    next_input = from_behind(mixed, "section", 1)
    input_grad = (here + from_down.astype(F32) + from_up.astype(F32)).astype(BF)
    prev_grad = from_behind(input_grad, "section", -1)
    return (
        next_input[None, None],
        prev_grad[None, None],
        gate_total[None, None],
        up_total[None, None],
        down_total[None, None],
    )


def solution(mesh):
    return jax.shard_map(
        local,
        mesh=mesh,
        in_specs=(
            P("section", "dp", "expert", None),
            P("section", "dp", "expert", None),
            P("section", "dp", "expert", None),
            P("section", "dp", "expert", None),
            P("section", "expert", None, "dp"),
            P("section", "expert", None, "dp"),
            P("section", "expert", "dp", None),
        ),
        out_specs=(
            P("section", "dp", "expert", None),
            P("section", "dp", "expert", None),
            P("section", "expert", None, "dp"),
            P("section", "expert", None, "dp"),
            P("section", "expert", "dp", None),
        ),
        check_vma=False,
    )
```

```python
import jax
import jax.numpy as jnp
from jax import lax
from jax.experimental import pallas as pl
from jax.experimental.pallas import tpu as pltpu
from jax.sharding import PartitionSpec as P

GROUP = ("expert", "dp")
BF = jnp.bfloat16
F32 = jnp.float32


def place(y, z, c):
    return (((y * 2 + z % 2) * 2 + c) * 2) + z // 2


def shifted(x, dy, dz, dc):
    pairs = [
        (place(y, z, c), place((y + dy) % 4, (z + dz) % 4, c ^ dc))
        for y in range(4)
        for z in range(4)
        for c in range(2)
    ]
    return lax.ppermute(x, GROUP, pairs)


def shift_y(x, by):
    return x if by % 4 == 0 else shifted(x, by, 0, 0)


def shift_z(x, by):
    return x if by % 4 == 0 else shifted(x, 0, by, 0)


def swap_core(x):
    return shifted(x, 0, 0, 1)


def after(x, done):
    return lax.optimization_barrier((x, done))[0]


def from_behind(x, axis, by):
    count = lax.axis_size(axis)
    pairs = [(i, i + by) for i in range(count) if 0 <= i + by < count]
    return lax.ppermute(x, axis, pairs)


def slot_codes(ids, experts, slot_rows):
    rows = ids.shape[-2]
    onehot = (ids[..., None] == jnp.arange(experts, dtype=F32)).astype(F32)
    named = jnp.sum(onehot, axis=-2).astype(BF)
    before = jnp.tri(rows, k=-1, dtype=BF)
    earlier = jnp.einsum("ij,...je->...ie", before, named, preferred_element_type=F32)
    position = jnp.sum(onehot * earlier[..., None, :], axis=-1)
    return (ids * slot_rows + position).astype(jnp.int32)


def chosen(codes, weights, targets):
    hits = [codes[..., k, None] == targets for k in range(codes.shape[-1])]
    weight = sum(jnp.sum(jnp.where(h, weights[..., k, None], 0.0), axis=-2) for k, h in enumerate(hits))
    return [h.astype(BF) for h in hits], hits[0].astype(BF) + hits[1].astype(BF), weight


def in_three(w):
    high = lax.reduce_precision(w, 8, 7)
    middle = lax.reduce_precision(w - high, 8, 7)
    return high, middle, w - high - middle


def mm(a, b):
    return jnp.dot(a, b, preferred_element_type=F32)


def mm_last(a, b):
    return lax.dot_general(a, b, (((1,), (1,)), ((), ())), preferred_element_type=F32)


def mm_first(a, b):
    return lax.dot_general(a, b, (((0,), (0,)), ((), ())), preferred_element_type=F32)


def kernel_call(body, grid, in_specs, out_specs, out_shape, scratch=()):
    return pl.pallas_call(
        body,
        grid=(grid,),
        in_specs=in_specs,
        out_specs=out_specs,
        out_shape=out_shape,
        scratch_shapes=scratch,
        compiler_params=pltpu.CompilerParams(vmem_limit_bytes=40 * 1024 * 1024),
        cost_estimate=pl.CostEstimate(flops=1, bytes_accessed=1, transcendentals=0),
    )


def whole(x):
    return pl.BlockSpec(x.shape, lambda i: (0, 0))


def columns(rows, n):
    return pl.BlockSpec((rows, n), lambda i: (0, i))


def rows_block(n, width):
    return pl.BlockSpec((n, width), lambda i: (i, 0))


def forward(pieces, gate_matrix, up_matrix):
    count, rows = len(pieces), pieces[0].shape[0]
    depth, units = gate_matrix.shape
    n = units // 2

    def body(*refs):
        gate, up, outs = refs[count], refs[count + 1], refs[count + 2 :]
        for i in range(count):
            x = refs[i][...]
            g, u = mm(x, gate[...]), mm(x, up[...])
            outs[3 * i][...] = g
            outs[3 * i + 1][...] = u
            outs[3 * i + 2][...] = (g * jax.nn.sigmoid(g) * u).astype(BF)

    shapes = [jax.ShapeDtypeStruct((rows, units), t) for t in (F32, F32, BF)] * count
    outs = kernel_call(
        body,
        2,
        [whole(x) for x in pieces] + [columns(depth, n)] * 2,
        [columns(rows, n)] * (3 * count),
        shapes,
    )(*pieces, gate_matrix, up_matrix)
    return [outs[3 * i : 3 * i + 3] for i in range(count)]


def outputs(hidden, down_matrix):
    count, rows = len(hidden), hidden[0].shape[0]
    units, width = down_matrix.shape
    n = width // 7

    def body(*refs):
        for i in range(count):
            refs[count + 1 + i][...] = mm(refs[i][...], refs[count][...]).astype(BF)

    return kernel_call(
        body,
        7,
        [whole(h) for h in hidden] + [columns(units, n)],
        [columns(rows, n)] * count,
        [jax.ShapeDtypeStruct((rows, width), BF)] * count,
    )(*hidden, down_matrix)


def hidden_grads(pieces, down_matrix):
    count, rows = len(pieces), pieces[0].shape[0]
    units, width = down_matrix.shape
    n = units // 2

    def body(*refs):
        for i in range(count):
            refs[count + 1 + i][...] = mm_last(refs[i][...], refs[count][...])

    return kernel_call(
        body,
        2,
        [whole(g) for g in pieces] + [rows_block(n, width)],
        [columns(rows, n)] * count,
        [jax.ShapeDtypeStruct((rows, units), F32)] * count,
    )(*pieces, down_matrix)


def backward(groups, slot, gate_pre, up_pre, hidden_grad, gate_matrix, up_matrix):
    used_s = sorted({s for _, those in groups for s in those})
    pairs = sorted((s, t) for t, those in groups for s in those)
    rows, units = gate_pre[used_s[0]].shape
    width = gate_matrix.shape[0]
    n = width // 7
    counts = [2 * len(those) * slot for _, those in groups]
    starts = [sum(counts[:i]) for i in range(len(groups))]
    total = sum(counts)
    many, those_s = len(groups), len(used_s)

    def body(*refs):
        gates = dict(zip(used_s, refs[:those_s]))
        ups = dict(zip(used_s, refs[those_s : 2 * those_s]))
        refs = refs[2 * those_s :]
        grads, (gate, up), refs = refs[:many], refs[many : many + 2], refs[many + 2 :]
        backs, (gate_out, up_out, gate_rows, up_rows) = refs[:many], refs[many:]

        @pl.when(pl.program_id(0) == 0)
        def _():
            for i, (t, those) in enumerate(groups):
                terms = {}
                for d in range(2):
                    for s in those:
                        here = pl.ds((t * 2 + d) * slot, slot)
                        g, u = gates[s][here, :], ups[s][here, :]
                        h = grads[i][pl.ds((d * 4 + s) * slot, slot), :]
                        sig = jax.nn.sigmoid(g)
                        terms[d, s] = (h * u * sig * (1.0 + g * (1.0 - sig)), h * g * sig)
                order = [terms[d, s] for d in range(2) for s in those]
                for which, by_t, by_s in ((0, gate_rows, gate_out), (1, up_rows, up_out)):
                    for k in range(0, len(order), 2):
                        pair = jnp.concatenate([order[k][which], order[k + 1][which]], axis=0)
                        by_t[pl.ds(starts[i] + k * slot, 2 * slot), :] = pair.astype(BF)
                    for s in those:
                        pair = jnp.concatenate([terms[0, s][which], terms[1, s][which]], axis=0)
                        by_s[pl.ds(pairs.index((s, t)) * 2 * slot, 2 * slot), :] = pair.astype(BF)

        back = mm_last(gate_rows[...], gate[...]) + mm_last(up_rows[...], up[...])
        for i in range(many):
            backs[i][...] = back[starts[i] : starts[i] + counts[i]].astype(BF)

    both = jax.ShapeDtypeStruct((total, units), BF)
    operands = [gate_pre[s] for s in used_s] + [up_pre[s] for s in used_s]
    operands += [hidden_grad[t] for t, _ in groups]
    outs = kernel_call(
        body,
        7,
        [whole(a) for a in operands] + [rows_block(n, units)] * 2,
        [columns(count, n) for count in counts] + [whole(both)] * 2,
        [jax.ShapeDtypeStruct((count, width), BF) for count in counts] + [both] * 2,
        [pltpu.VMEM(both.shape, BF)] * 2,
    )(*operands, gate_matrix, up_matrix)
    grads = [
        {pair: a[k * 2 * slot : (k + 1) * 2 * slot] for k, pair in enumerate(pairs)} for a in outs[many:]
    ]
    return outs[:many], grads[0], grads[1]


def local(tokens, grad_out, expert_ids, route_weight, w_gate, w_up, w_down):
    inputs = tokens[0, 0]
    upstream = grad_out[0, 0]
    weights = route_weight[0, 0]
    gate_matrix, up_matrix, down_matrix = w_gate[0, 0], w_up[0, 0], w_down[0, 0]
    experts = lax.axis_size("expert")
    rows, per_token = weights.shape
    width = inputs.shape[1]
    split = rows // 2
    slot = 3 * rows * per_token // (2 * experts)
    flat = 8 * slot
    me = lax.axis_index("expert")
    y, zl, c = me // 4, (me // 2) % 2, me % 2

    ids = expert_ids[0, 0].astype(F32)
    fields = [ids] + [jnp.stack([a[:, k] for a in in_three(weights)], axis=1) for k in range(per_token)]
    fields = jnp.concatenate(fields, axis=1).astype(BF)
    codes = slot_codes(ids, experts, slot)
    step = jnp.arange(4, dtype=jnp.int32)
    two = jnp.arange(2, dtype=jnp.int32)
    slots = jnp.arange(slot, dtype=jnp.int32)
    dest_y = ((y + step) % 4) * 4
    targets_z = (
        (dest_y[None, :, None] + zl * 2 + (c ^ two)[:, None, None]) * slot + slots
    ).reshape(-1)
    targets_y = (
        (
            dest_y[None, :, None, None]
            + (zl ^ two)[None, None, :, None] * 2
            + (c ^ two)[:, None, None, None]
        )
        * slot
        + slots
    ).reshape(-1)
    each_y, pick_y, _ = chosen(codes, weights, targets_y)
    own, sib = [
        mm_first(pick_y[:, dc * flat : (dc + 1) * flat], inputs).astype(BF) for dc in range(2)
    ]
    message = jnp.concatenate(
        [after(upstream, sib), jnp.pad(fields.T, ((0, 0), (0, width - rows)))], axis=0
    )
    near1, near3 = shift_z(message, 1), shift_z(message, 3)
    sib = swap_core(sib)
    along_y = [
        jnp.concatenate([a[t * 2 * slot : (t + 1) * 2 * slot] for a in (own, sib)]) for t in range(4)
    ]
    y1, y3 = shift_y(along_y[1], 1), shift_y(along_y[3], 3)

    near1, near3, y1, y3, far_y = lax.optimization_barrier((near1, near3, y1, y3, along_y[2]))
    y2 = shift_y(far_y, 2)
    far_a, far_b = shift_z(near1[:split], 1), shift_z(near3[split:], 3)
    ring_tables = [fields, near1[rows:, :rows].T, far_b[rows - split :, :rows].T, near3[rows:, :rows].T]

    def picks(table):
        table = table.astype(F32)
        parts = [table[:, per_token + 3 * k : per_token + 3 * k + 3] for k in range(per_token)]
        weigh = jnp.stack([p[:, 0] + p[:, 1] + p[:, 2] for p in parts], axis=-1)
        return chosen(slot_codes(table[:, :per_token], experts, slot), weigh, targets_z)[1:]

    pick_z, slot_weight_z = zip(*[picks(a) for a in ring_tables])
    far_a, far_b, near1, near3, late_upstream = lax.optimization_barrier(
        (far_a, far_b, near1, near3, upstream)
    )
    far = jnp.concatenate([far_a, far_b[: rows - split]])
    sel = [
        (slot_weight_z[s][:, None] * mm_first(pick_z[s], block)).astype(BF).reshape(2, 4, slot, width)
        for s, block in enumerate((late_upstream, near1[:rows], far, near3[:rows]))
    ]
    cross = [jnp.stack([a[1, t] for t in those for a in sel]) for those in ((1, 3), (0, 2))]

    sel, cross, y1, y2, y3 = lax.optimization_barrier((sel, cross, y1, y2, y3))
    by_y = [along_y[0], y1, y2, y3]
    same, other = [
        jnp.concatenate([a[k * slot : (k + 1) * slot] for a in by_y for k in (dl, 2 + dl)])
        for dl in range(2)
    ]
    x1, x3 = shift_z(other, 1), shift_z(other, 3)
    odd, even = swap_core(cross[0]), swap_core(cross[1])
    sib = [even[:4], odd[:4], even[4:], odd[4:]]
    out_y = [
        jnp.concatenate([jnp.stack([sel[s][0, t] for s in range(4)]), sib[t]]).reshape(flat, width)
        for t in range(4)
    ]
    g1, g3 = shift_y(out_y[1], 1), shift_y(out_y[3], 3)

    x1, x3, g1, g3, same_far, out_far = lax.optimization_barrier((x1, x3, g1, g3, same, out_y[2]))
    x2, g2 = shift_z(same_far, 2), shift_y(out_far, 2)
    ahead = forward([x1, x3, same_far], gate_matrix, up_matrix)
    out1, out3 = outputs([ahead[0][2], ahead[1][2]], down_matrix)
    grad1, grad3, grad0 = hidden_grads([g1, g3, out_y[0]], down_matrix)
    gate_pre, up_pre, hidden = [{0: ahead[2][i], 1: ahead[0][i], 3: ahead[1][i]} for i in range(3)]
    early = ((1, (0, 1, 3)), (3, (0, 1, 3)))
    (back1, back3), gate_grad, up_grad = backward(
        early, slot, gate_pre, up_pre, {1: grad1, 3: grad3}, gate_matrix, up_matrix
    )

    x2, g2, out1, out3, back1, back3 = lax.optimization_barrier((x2, g2, out1, out3, back1, back3))
    e1, e3 = shift_z(out1, -1), shift_z(out3, -3)
    b1, b3 = shift_y(back1, -1), shift_y(back3, -3)
    ((gate_pre[2], up_pre[2], hidden[2]),) = forward([x2], gate_matrix, up_matrix)
    (grad2,) = hidden_grads([g2], down_matrix)
    out2, out0 = outputs([hidden[2], hidden[0]], down_matrix)
    rest = ((0, (0, 1, 2, 3)), (2, (0, 1, 2, 3)), (1, (2,)), (3, (2,)))
    (back0, back2, back1, back3), more_gate, more_up = backward(
        rest,
        slot,
        gate_pre,
        up_pre,
        {0: grad0, 1: grad1, 2: grad2, 3: grad3},
        gate_matrix,
        up_matrix,
    )
    gate_grad, up_grad = {**gate_grad, **more_gate}, {**up_grad, **more_up}

    e1, e3, b1, b3, out0, out2, back0, back1, back2, back3 = lax.optimization_barrier(
        (e1, e3, b1, b3, out0, out2, back0, back1, back2, back3)
    )
    e2, b2 = shift_z(out2, -2), shift_y(back2, -2)
    far1, far3 = shift_y(back1, -1), shift_y(back3, -3)
    swapped = swap_core(back0[4 * slot :])
    back0 = back0.reshape(2, 4, slot, width)
    b1, b3 = [a.reshape(2, 3, slot, width) for a in (b1, b3)]
    late_g, late_hidden, _ = lax.optimization_barrier(((out_y[0], g1, g2, g3), hidden, e1))
    late_hidden = jnp.stack([late_hidden[s].reshape(4, 2, slot, -1) for s in range(4)], axis=2)
    down_total = mm_first(late_hidden.reshape(4 * flat, -1), jnp.concatenate(late_g)).astype(BF)

    e1, e2, e3, b2, far1, far3, swapped = lax.optimization_barrier(
        (e1, e2, e3, b2, far1, far3, swapped)
    )
    swapped = swapped.reshape(4, slot, width)
    b2 = b2.reshape(2, 4, slot, width)
    far1, far3 = [a.reshape(2, 1, slot, width) for a in (far1, far3)]
    others = swap_core(jnp.concatenate([b2[1], b1[1], b3[1], far1[1], far3[1]]))

    def in_order(whole0, part1, whole2, part3, rest1, rest3):
        part1, part3 = [[p[0], p[1], r[0], p[2]] for p, r in ((part1, rest1), (part3, rest3))]
        return [whole0, part1, whole2, part3]

    back = [
        in_order(back0[0], b1[0], b2[0], b3[0], far1[0], far3[0]),
        in_order(swapped, others[4:7], others[:4], others[7:10], others[10:11], others[11:]),
    ]

    def by_token(s):
        rows_of = jnp.stack([back[dc][t][s] for dc in range(2) for t in range(4)])
        return mm(pick_z[s], rows_of.reshape(-1, width))

    both = [
        (out0.astype(F32) + e2.astype(F32)).astype(BF).reshape(4, 2, slot, width),
        (e1.astype(F32) + e3.astype(F32)).astype(BF).reshape(4, 2, slot, width),
    ]
    both = [jnp.stack([a[t] for a in both]) for t in range(4)]
    m1, m3 = shift_y(both[1], -1), shift_y(both[3], -3)
    far = by_token(2).astype(BF)
    far_a, far_b = shift_z(far[:split], 1), shift_z(far[split:], -1)
    up_z, down_z, here = by_token(3), by_token(1), by_token(0)

    far_a, far_b, m1, m3, both_far = lax.optimization_barrier((far_a, far_b, m1, m3, both[2]))
    up_z = jnp.concatenate([up_z[:split] + far_a.astype(F32), up_z[split:]]).astype(BF)
    down_z = jnp.concatenate([down_z[:split], down_z[split:] + far_b.astype(F32)]).astype(BF)
    from_down, from_up = shift_z(up_z, 1), shift_z(down_z, -1)
    m2 = shift_y(both_far, -2)
    swapped = swap_core(jnp.stack([both[0][:, 1], m1[:, 1], m3[:, 1]]))
    late_x, late_gate, _ = lax.optimization_barrier(((same, x1, x2, x3), gate_grad, far_a))

    def by_s(grads):
        return jnp.concatenate([grads[s, t] for s in range(4) for t in range(4)])

    late_x = jnp.concatenate(late_x)
    gate_total = mm_first(late_x, by_s(late_gate)).astype(BF)

    sib = [swapped[0], swapped[1], swap_core(m2[:, 1]), swapped[2]]
    back = jnp.stack([both[0][:, 0], m1[:, 0], m2[:, 0], m3[:, 0]] + sib).reshape(-1, width)
    mixed = sum(weights[:, k, None] * mm(each_y[k], back) for k in range(per_token)).astype(BF)
    next_input = from_behind(mixed, "section", 1)
    input_grad = (here + from_down.astype(F32) + from_up.astype(F32)).astype(BF)
    prev_grad = from_behind(input_grad, "section", -1)
    late_x, late_up, _ = lax.optimization_barrier((late_x, up_grad, m2))
    up_total = mm_first(late_x, by_s(late_up)).astype(BF)
    return (
        next_input[None, None],
        prev_grad[None, None],
        gate_total[None, None],
        up_total[None, None],
        down_total[None, None],
    )


def solution(mesh):
    return jax.shard_map(
        local,
        mesh=mesh,
        in_specs=(
            P("section", "dp", "expert", None),
            P("section", "dp", "expert", None),
            P("section", "dp", "expert", None),
            P("section", "dp", "expert", None),
            P("section", "expert", None, "dp"),
            P("section", "expert", None, "dp"),
            P("section", "expert", "dp", None),
        ),
        out_specs=(
            P("section", "dp", "expert", None),
            P("section", "dp", "expert", None),
            P("section", "expert", None, "dp"),
            P("section", "expert", None, "dp"),
            P("section", "expert", "dp", None),
        ),
        check_vma=False,
    )
```

```python
import jax
import jax.numpy as jnp
from jax import lax
from jax.experimental import pallas as pl
from jax.experimental.pallas import tpu as pltpu
from jax.sharding import PartitionSpec as P

GROUP = ("expert", "dp")
BF = jnp.bfloat16
F32 = jnp.float32


def place(y, z, c):
    return (((y * 2 + z % 2) * 2 + c) * 2) + z // 2


def shifted(x, dy, dz, dc):
    pairs = [
        (place(y, z, c), place((y + dy) % 4, (z + dz) % 4, c ^ dc))
        for y in range(4)
        for z in range(4)
        for c in range(2)
    ]
    return lax.ppermute(x, GROUP, pairs)


def shift_y(x, by):
    return x if by % 4 == 0 else shifted(x, by, 0, 0)


def shift_z(x, by):
    return x if by % 4 == 0 else shifted(x, 0, by, 0)


def swap_core(x):
    return shifted(x, 0, 0, 1)


def after(x, done):
    return lax.optimization_barrier((x, done))[0]


def from_behind(x, axis, by):
    count = lax.axis_size(axis)
    pairs = [(i, i + by) for i in range(count) if 0 <= i + by < count]
    return lax.ppermute(x, axis, pairs)


def slot_codes(ids, experts, slot_rows):
    rows = ids.shape[-2]
    onehot = (ids[..., None] == jnp.arange(experts, dtype=F32)).astype(F32)
    named = jnp.sum(onehot, axis=-2).astype(BF)
    before = jnp.tri(rows, k=-1, dtype=BF)
    earlier = jnp.einsum("ij,...je->...ie", before, named, preferred_element_type=F32)
    position = jnp.sum(onehot * earlier[..., None, :], axis=-1)
    return (ids * slot_rows + position).astype(jnp.int32)


def chosen(codes, weights, targets):
    hits = [codes[..., k, None] == targets for k in range(codes.shape[-1])]
    weight = sum(jnp.sum(jnp.where(h, weights[..., k, None], 0.0), axis=-2) for k, h in enumerate(hits))
    return [h.astype(BF) for h in hits], hits[0].astype(BF) + hits[1].astype(BF), weight


def in_three(w):
    high = lax.reduce_precision(w, 8, 7)
    middle = lax.reduce_precision(w - high, 8, 7)
    return high, middle, w - high - middle


def mm(a, b):
    return jnp.dot(a, b, preferred_element_type=F32)


def mm_last(a, b):
    return lax.dot_general(a, b, (((1,), (1,)), ((), ())), preferred_element_type=F32)


def mm_first(a, b):
    return lax.dot_general(a, b, (((0,), (0,)), ((), ())), preferred_element_type=F32)


def kernel_call(body, grid, in_specs, out_specs, out_shape, scratch=()):
    return pl.pallas_call(
        body,
        grid=(grid,),
        in_specs=in_specs,
        out_specs=out_specs,
        out_shape=out_shape,
        scratch_shapes=scratch,
        compiler_params=pltpu.CompilerParams(vmem_limit_bytes=40 * 1024 * 1024),
        cost_estimate=pl.CostEstimate(flops=1, bytes_accessed=1, transcendentals=0),
    )


def whole(x):
    return pl.BlockSpec(x.shape, lambda i: (0, 0))


def columns(rows, n):
    return pl.BlockSpec((rows, n), lambda i: (0, i))


def rows_block(n, width):
    return pl.BlockSpec((n, width), lambda i: (i, 0))


def forward(pieces, gate_matrix, up_matrix):
    count, rows = len(pieces), pieces[0].shape[0]
    depth, units = gate_matrix.shape
    n = units // 2

    def body(*refs):
        gate, up, outs = refs[count], refs[count + 1], refs[count + 2 :]
        for i in range(count):
            x = refs[i][...]
            g, u = mm(x, gate[...]), mm(x, up[...])
            outs[3 * i][...] = g
            outs[3 * i + 1][...] = u
            outs[3 * i + 2][...] = (g * jax.nn.sigmoid(g) * u).astype(BF)

    shapes = [jax.ShapeDtypeStruct((rows, units), t) for t in (F32, F32, BF)] * count
    outs = kernel_call(
        body,
        2,
        [whole(x) for x in pieces] + [columns(depth, n)] * 2,
        [columns(rows, n)] * (3 * count),
        shapes,
    )(*pieces, gate_matrix, up_matrix)
    return [outs[3 * i : 3 * i + 3] for i in range(count)]


def outputs(hidden, down_matrix):
    count, rows = len(hidden), hidden[0].shape[0]
    units, width = down_matrix.shape
    n = width // 7

    def body(*refs):
        for i in range(count):
            refs[count + 1 + i][...] = mm(refs[i][...], refs[count][...]).astype(BF)

    return kernel_call(
        body,
        7,
        [whole(h) for h in hidden] + [columns(units, n)],
        [columns(rows, n)] * count,
        [jax.ShapeDtypeStruct((rows, width), BF)] * count,
    )(*hidden, down_matrix)


def hidden_grads(pieces, down_matrix):
    count, rows = len(pieces), pieces[0].shape[0]
    units, width = down_matrix.shape
    n = units // 2

    def body(*refs):
        for i in range(count):
            refs[count + 1 + i][...] = mm_last(refs[i][...], refs[count][...])

    return kernel_call(
        body,
        2,
        [whole(g) for g in pieces] + [rows_block(n, width)],
        [columns(rows, n)] * count,
        [jax.ShapeDtypeStruct((rows, units), F32)] * count,
    )(*pieces, down_matrix)


def backward(groups, slot, gate_pre, up_pre, hidden_grad, gate_matrix, up_matrix):
    used_s = sorted({s for _, those in groups for s in those})
    pairs = sorted((s, t) for t, those in groups for s in those)
    rows, units = gate_pre[used_s[0]].shape
    width = gate_matrix.shape[0]
    n = width // 7
    counts = [2 * len(those) * slot for _, those in groups]
    starts = [sum(counts[:i]) for i in range(len(groups))]
    total = sum(counts)
    many, those_s = len(groups), len(used_s)

    def body(*refs):
        gates = dict(zip(used_s, refs[:those_s]))
        ups = dict(zip(used_s, refs[those_s : 2 * those_s]))
        refs = refs[2 * those_s :]
        grads, (gate, up), refs = refs[:many], refs[many : many + 2], refs[many + 2 :]
        backs, (gate_out, up_out, gate_rows, up_rows) = refs[:many], refs[many:]

        @pl.when(pl.program_id(0) == 0)
        def _():
            for i, (t, those) in enumerate(groups):
                terms = {}
                for d in range(2):
                    for s in those:
                        here = pl.ds((t * 2 + d) * slot, slot)
                        g, u = gates[s][here, :], ups[s][here, :]
                        h = grads[i][pl.ds((d * 4 + s) * slot, slot), :]
                        sig = jax.nn.sigmoid(g)
                        terms[d, s] = (h * u * sig * (1.0 + g * (1.0 - sig)), h * g * sig)
                order = [terms[d, s] for d in range(2) for s in those]
                for which, by_t, by_s in ((0, gate_rows, gate_out), (1, up_rows, up_out)):
                    for k in range(0, len(order), 2):
                        pair = jnp.concatenate([order[k][which], order[k + 1][which]], axis=0)
                        by_t[pl.ds(starts[i] + k * slot, 2 * slot), :] = pair.astype(BF)
                    for s in those:
                        pair = jnp.concatenate([terms[0, s][which], terms[1, s][which]], axis=0)
                        by_s[pl.ds(pairs.index((s, t)) * 2 * slot, 2 * slot), :] = pair.astype(BF)

        back = mm_last(gate_rows[...], gate[...]) + mm_last(up_rows[...], up[...])
        for i in range(many):
            backs[i][...] = back[starts[i] : starts[i] + counts[i]].astype(BF)

    both = jax.ShapeDtypeStruct((total, units), BF)
    operands = [gate_pre[s] for s in used_s] + [up_pre[s] for s in used_s]
    operands += [hidden_grad[t] for t, _ in groups]
    outs = kernel_call(
        body,
        7,
        [whole(a) for a in operands] + [rows_block(n, units)] * 2,
        [columns(count, n) for count in counts] + [whole(both)] * 2,
        [jax.ShapeDtypeStruct((count, width), BF) for count in counts] + [both] * 2,
        [pltpu.VMEM(both.shape, BF)] * 2,
    )(*operands, gate_matrix, up_matrix)
    grads = [
        {pair: a[k * 2 * slot : (k + 1) * 2 * slot] for k, pair in enumerate(pairs)} for a in outs[many:]
    ]
    return outs[:many], grads[0], grads[1]


def local(tokens, grad_out, expert_ids, route_weight, w_gate, w_up, w_down):
    inputs = tokens[0, 0]
    upstream = grad_out[0, 0]
    weights = route_weight[0, 0]
    gate_matrix, up_matrix, down_matrix = w_gate[0, 0], w_up[0, 0], w_down[0, 0]
    experts = lax.axis_size("expert")
    rows, per_token = weights.shape
    width = inputs.shape[1]
    split = rows // 2
    slot = 3 * rows * per_token // (2 * experts)
    flat = 8 * slot
    me = lax.axis_index("expert")
    y, zl, c = me // 4, (me // 2) % 2, me % 2

    ids = expert_ids[0, 0].astype(F32)
    fields = [ids] + [jnp.stack([a[:, k] for a in in_three(weights)], axis=1) for k in range(per_token)]
    fields = jnp.concatenate(fields, axis=1).astype(BF)
    codes = slot_codes(ids, experts, slot)
    step = jnp.arange(4, dtype=jnp.int32)
    two = jnp.arange(2, dtype=jnp.int32)
    slots = jnp.arange(slot, dtype=jnp.int32)
    dest_y = ((y + step) % 4) * 4
    targets_z = (
        (dest_y[None, :, None] + zl * 2 + (c ^ two)[:, None, None]) * slot + slots
    ).reshape(-1)
    targets_y = (
        (
            dest_y[None, :, None, None]
            + (zl ^ two)[None, None, :, None] * 2
            + (c ^ two)[:, None, None, None]
        )
        * slot
        + slots
    ).reshape(-1)
    each_y, pick_y, _ = chosen(codes, weights, targets_y)
    own, sib = [
        mm_first(pick_y[:, dc * flat : (dc + 1) * flat], inputs).astype(BF) for dc in range(2)
    ]
    message = jnp.concatenate(
        [after(upstream, sib), jnp.pad(fields.T, ((0, 0), (0, width - rows)))], axis=0
    )
    near1, near3 = shift_z(message, 1), shift_z(message, 3)
    sib = swap_core(sib)
    along_y = [
        jnp.concatenate([a[t * 2 * slot : (t + 1) * 2 * slot] for a in (own, sib)]) for t in range(4)
    ]
    y1, y3 = shift_y(along_y[1], 1), shift_y(along_y[3], 3)

    near1, near3, y1, y3, far_y = lax.optimization_barrier((near1, near3, y1, y3, along_y[2]))
    y2 = shift_y(far_y, 2)
    far_a, far_b = shift_z(near1[:split], 1), shift_z(near3[split:], 3)
    ring_tables = [fields, near1[rows:, :rows].T, far_b[rows - split :, :rows].T, near3[rows:, :rows].T]

    def picks(table):
        table = table.astype(F32)
        parts = [table[:, per_token + 3 * k : per_token + 3 * k + 3] for k in range(per_token)]
        weigh = jnp.stack([p[:, 0] + p[:, 1] + p[:, 2] for p in parts], axis=-1)
        return chosen(slot_codes(table[:, :per_token], experts, slot), weigh, targets_z)[1:]

    pick_z, slot_weight_z = zip(*[picks(a) for a in ring_tables])
    far_a, far_b, near1, near3, late_upstream = lax.optimization_barrier(
        (far_a, far_b, near1, near3, upstream)
    )
    far = jnp.concatenate([far_a, far_b[: rows - split]])
    sel = [
        (slot_weight_z[s][:, None] * mm_first(pick_z[s], block)).astype(BF).reshape(2, 4, slot, width)
        for s, block in enumerate((late_upstream, near1[:rows], far, near3[:rows]))
    ]
    cross = [jnp.stack([a[1, t] for t in those for a in sel]) for those in ((1, 3), (0, 2))]

    sel, cross, y1, y2, y3 = lax.optimization_barrier((sel, cross, y1, y2, y3))
    by_y = [along_y[0], y1, y2, y3]
    same, other = [
        jnp.concatenate([a[k * slot : (k + 1) * slot] for a in by_y for k in (dl, 2 + dl)])
        for dl in range(2)
    ]
    x1, x3 = shift_z(other, 1), shift_z(other, 3)
    odd, even = swap_core(cross[0]), swap_core(cross[1])
    sib = [even[:4], odd[:4], even[4:], odd[4:]]
    out_y = [
        jnp.concatenate([jnp.stack([sel[s][0, t] for s in range(4)]), sib[t]]).reshape(flat, width)
        for t in range(4)
    ]
    g1, g3 = shift_y(out_y[1], 1), shift_y(out_y[3], 3)

    x1, x3, g1, g3, same_far, out_far = lax.optimization_barrier((x1, x3, g1, g3, same, out_y[2]))
    x2, g2 = shift_z(same_far, 2), shift_y(out_far, 2)
    ahead = forward([x1, x3, same_far], gate_matrix, up_matrix)
    out1, out3 = outputs([ahead[0][2], ahead[1][2]], down_matrix)
    grad1, grad3, grad0 = hidden_grads([g1, g3, out_y[0]], down_matrix)
    gate_pre, up_pre, hidden = [{0: ahead[2][i], 1: ahead[0][i], 3: ahead[1][i]} for i in range(3)]
    early = ((1, (0, 1, 3)), (3, (0, 1, 3)))
    (back1, back3), gate_grad, up_grad = backward(
        early, slot, gate_pre, up_pre, {1: grad1, 3: grad3}, gate_matrix, up_matrix
    )

    x2, g2, out1, out3, back1, back3 = lax.optimization_barrier((x2, g2, out1, out3, back1, back3))
    e1, e3 = shift_z(out1, -1), shift_z(out3, -3)
    b1, b3 = shift_y(back1, -1), shift_y(back3, -3)
    ((gate_pre[2], up_pre[2], hidden[2]),) = forward([x2], gate_matrix, up_matrix)
    (grad2,) = hidden_grads([g2], down_matrix)
    out2, out0 = outputs([hidden[2], hidden[0]], down_matrix)
    rest = ((0, (0, 1, 2, 3)), (2, (0, 1, 2, 3)), (1, (2,)), (3, (2,)))
    (back0, back2, back1, back3), more_gate, more_up = backward(
        rest,
        slot,
        gate_pre,
        up_pre,
        {0: grad0, 1: grad1, 2: grad2, 3: grad3},
        gate_matrix,
        up_matrix,
    )
    gate_grad, up_grad = {**gate_grad, **more_gate}, {**up_grad, **more_up}

    e1, e3, b1, b3, out0, out2, back0, back1, back2, back3 = lax.optimization_barrier(
        (e1, e3, b1, b3, out0, out2, back0, back1, back2, back3)
    )
    e2, b2 = shift_z(out2, -2), shift_y(back2, -2)
    far1, far3 = shift_y(back1, -1), shift_y(back3, -3)
    swapped = swap_core(back0[4 * slot :])
    back0 = back0.reshape(2, 4, slot, width)
    b1, b3 = [a.reshape(2, 3, slot, width) for a in (b1, b3)]
    late_g, late_hidden, _ = lax.optimization_barrier(((out_y[0], g1, g2, g3), hidden, e1))
    late_hidden = jnp.stack([late_hidden[s].reshape(4, 2, slot, -1) for s in range(4)], axis=2)
    down_total = mm_first(late_hidden.reshape(4 * flat, -1), jnp.concatenate(late_g)).astype(BF)

    e1, e2, e3, b2, far1, far3, swapped = lax.optimization_barrier(
        (e1, e2, e3, b2, far1, far3, swapped)
    )
    swapped = swapped.reshape(4, slot, width)
    b2 = b2.reshape(2, 4, slot, width)
    far1, far3 = [a.reshape(2, 1, slot, width) for a in (far1, far3)]
    others = swap_core(jnp.concatenate([b2[1], b1[1], b3[1], far1[1], far3[1]]))

    both = [
        (out0.astype(F32) + e2.astype(F32)).astype(BF).reshape(4, 2, slot, width),
        (e1.astype(F32) + e3.astype(F32)).astype(BF).reshape(4, 2, slot, width),
    ]
    both, others = lax.optimization_barrier(
        ([jnp.stack([a[t] for a in both]) for t in range(4)], others)
    )

    def in_order(whole0, part1, whole2, part3, rest1, rest3):
        part1, part3 = [[p[0], p[1], r[0], p[2]] for p, r in ((part1, rest1), (part3, rest3))]
        return [whole0, part1, whole2, part3]

    back = [
        in_order(back0[0], b1[0], b2[0], b3[0], far1[0], far3[0]),
        in_order(swapped, others[4:7], others[:4], others[7:10], others[10:11], others[11:]),
    ]

    def by_token(s):
        rows_of = jnp.stack([back[dc][t][s] for dc in range(2) for t in range(4)])
        return mm(pick_z[s], rows_of.reshape(-1, width))

    m1, m3 = shift_y(both[1], -1), shift_y(both[3], -3)
    far = by_token(2).astype(BF)
    far_a, far_b = shift_z(far[:split], 1), shift_z(far[split:], -1)
    up_z, down_z, here = by_token(3), by_token(1), by_token(0)

    far_a, far_b, m1, m3, both_far = lax.optimization_barrier((far_a, far_b, m1, m3, both[2]))
    up_z = jnp.concatenate([up_z[:split] + far_a.astype(F32), up_z[split:]]).astype(BF)
    down_z = jnp.concatenate([down_z[:split], down_z[split:] + far_b.astype(F32)]).astype(BF)
    from_down, from_up = shift_z(up_z, 1), shift_z(down_z, -1)
    m2 = shift_y(both_far, -2)
    swapped = swap_core(jnp.stack([both[0][:, 1], m1[:, 1], m3[:, 1]]))
    late_x, late_gate, _ = lax.optimization_barrier(((same, x1, x2, x3), gate_grad, far_a))

    def by_s(grads):
        return jnp.concatenate([grads[s, t] for s in range(4) for t in range(4)])

    late_x = jnp.concatenate(late_x)
    gate_total = mm_first(late_x, by_s(late_gate)).astype(BF)

    sib = [swapped[0], swapped[1], swap_core(m2[:, 1]), swapped[2]]
    back = jnp.stack([both[0][:, 0], m1[:, 0], m2[:, 0], m3[:, 0]] + sib).reshape(-1, width)
    mixed = sum(weights[:, k, None] * mm(each_y[k], back) for k in range(per_token)).astype(BF)
    next_input = from_behind(mixed, "section", 1)
    input_grad = (here + from_down.astype(F32) + from_up.astype(F32)).astype(BF)
    prev_grad = from_behind(input_grad, "section", -1)
    late_x, late_up, _ = lax.optimization_barrier((late_x, up_grad, m2))
    up_total = mm_first(late_x, by_s(late_up)).astype(BF)
    return (
        next_input[None, None],
        prev_grad[None, None],
        gate_total[None, None],
        up_total[None, None],
        down_total[None, None],
    )


def solution(mesh):
    return jax.shard_map(
        local,
        mesh=mesh,
        in_specs=(
            P("section", "dp", "expert", None),
            P("section", "dp", "expert", None),
            P("section", "dp", "expert", None),
            P("section", "dp", "expert", None),
            P("section", "expert", None, "dp"),
            P("section", "expert", None, "dp"),
            P("section", "expert", "dp", None),
        ),
        out_specs=(
            P("section", "dp", "expert", None),
            P("section", "dp", "expert", None),
            P("section", "expert", None, "dp"),
            P("section", "expert", None, "dp"),
            P("section", "expert", "dp", None),
        ),
        check_vma=False,
    )
```

```python
import jax
import jax.numpy as jnp
from jax import lax
from jax.experimental import pallas as pl
from jax.experimental.pallas import tpu as pltpu
from jax.sharding import PartitionSpec as P

GROUP = ("expert", "dp")
BF = jnp.bfloat16
F32 = jnp.float32


def place(y, z, c):
    return (((y * 2 + z % 2) * 2 + c) * 2) + z // 2


def shifted(x, dy, dz, dc):
    pairs = [
        (place(y, z, c), place((y + dy) % 4, (z + dz) % 4, c ^ dc))
        for y in range(4)
        for z in range(4)
        for c in range(2)
    ]
    return lax.ppermute(x, GROUP, pairs)


def shift_y(x, by):
    return x if by % 4 == 0 else shifted(x, by, 0, 0)


def shift_z(x, by):
    return x if by % 4 == 0 else shifted(x, 0, by, 0)


def swap_core(x):
    return shifted(x, 0, 0, 1)


def after(x, done):
    return lax.optimization_barrier((x, done))[0]


def from_behind(x, axis, by):
    count = lax.axis_size(axis)
    pairs = [(i, i + by) for i in range(count) if 0 <= i + by < count]
    return lax.ppermute(x, axis, pairs)


def slot_codes(ids, experts, slot_rows):
    rows = ids.shape[-2]
    onehot = (ids[..., None] == jnp.arange(experts, dtype=F32)).astype(F32)
    named = jnp.sum(onehot, axis=-2).astype(BF)
    before = jnp.tri(rows, k=-1, dtype=BF)
    earlier = jnp.einsum("ij,...je->...ie", before, named, preferred_element_type=F32)
    position = jnp.sum(onehot * earlier[..., None, :], axis=-1)
    return (ids * slot_rows + position).astype(jnp.int32)


def chosen(codes, weights, targets):
    hits = [codes[..., k, None] == targets for k in range(codes.shape[-1])]
    weight = sum(jnp.sum(jnp.where(h, weights[..., k, None], 0.0), axis=-2) for k, h in enumerate(hits))
    return [h.astype(BF) for h in hits], hits[0].astype(BF) + hits[1].astype(BF), weight


def in_three(w):
    high = lax.reduce_precision(w, 8, 7)
    middle = lax.reduce_precision(w - high, 8, 7)
    return high, middle, w - high - middle


def mm(a, b):
    return jnp.dot(a, b, preferred_element_type=F32)


def mm_last(a, b):
    return lax.dot_general(a, b, (((1,), (1,)), ((), ())), preferred_element_type=F32)


def mm_first(a, b):
    return lax.dot_general(a, b, (((0,), (0,)), ((), ())), preferred_element_type=F32)


def kernel_call(body, grid, in_specs, out_specs, out_shape, scratch=()):
    return pl.pallas_call(
        body,
        grid=(grid,),
        in_specs=in_specs,
        out_specs=out_specs,
        out_shape=out_shape,
        scratch_shapes=scratch,
        compiler_params=pltpu.CompilerParams(vmem_limit_bytes=40 * 1024 * 1024),
        cost_estimate=pl.CostEstimate(flops=1, bytes_accessed=1, transcendentals=0),
    )


def whole(x):
    return pl.BlockSpec(x.shape, lambda i: (0, 0))


def columns(rows, n):
    return pl.BlockSpec((rows, n), lambda i: (0, i))


def rows_block(n, width):
    return pl.BlockSpec((n, width), lambda i: (i, 0))


def forward(pieces, gate_matrix, up_matrix):
    count, rows = len(pieces), pieces[0].shape[0]
    depth, units = gate_matrix.shape
    n = units // 2

    def body(*refs):
        gate, up, outs = refs[count], refs[count + 1], refs[count + 2 :]
        for i in range(count):
            x = refs[i][...]
            g, u = mm(x, gate[...]), mm(x, up[...])
            outs[3 * i][...] = g
            outs[3 * i + 1][...] = u
            outs[3 * i + 2][...] = (g * jax.nn.sigmoid(g) * u).astype(BF)

    shapes = [jax.ShapeDtypeStruct((rows, units), t) for t in (F32, F32, BF)] * count
    outs = kernel_call(
        body,
        2,
        [whole(x) for x in pieces] + [columns(depth, n)] * 2,
        [columns(rows, n)] * (3 * count),
        shapes,
    )(*pieces, gate_matrix, up_matrix)
    return [outs[3 * i : 3 * i + 3] for i in range(count)]


def outputs(hidden, down_matrix):
    count, rows = len(hidden), hidden[0].shape[0]
    units, width = down_matrix.shape
    n = width // 7

    def body(*refs):
        for i in range(count):
            refs[count + 1 + i][...] = mm(refs[i][...], refs[count][...]).astype(BF)

    return kernel_call(
        body,
        7,
        [whole(h) for h in hidden] + [columns(units, n)],
        [columns(rows, n)] * count,
        [jax.ShapeDtypeStruct((rows, width), BF)] * count,
    )(*hidden, down_matrix)


def hidden_grads(pieces, down_matrix):
    count, rows = len(pieces), pieces[0].shape[0]
    units, width = down_matrix.shape
    n = units // 2

    def body(*refs):
        for i in range(count):
            refs[count + 1 + i][...] = mm_last(refs[i][...], refs[count][...])

    return kernel_call(
        body,
        2,
        [whole(g) for g in pieces] + [rows_block(n, width)],
        [columns(rows, n)] * count,
        [jax.ShapeDtypeStruct((rows, units), F32)] * count,
    )(*pieces, down_matrix)


def backward(groups, slot, gate_pre, up_pre, hidden_grad, gate_matrix, up_matrix):
    used_s = sorted({s for _, those in groups for s in those})
    pairs = sorted((s, t) for t, those in groups for s in those)
    rows, units = gate_pre[used_s[0]].shape
    width = gate_matrix.shape[0]
    n = width // 7
    counts = [2 * len(those) * slot for _, those in groups]
    starts = [sum(counts[:i]) for i in range(len(groups))]
    total = sum(counts)
    many, those_s = len(groups), len(used_s)

    def body(*refs):
        gates = dict(zip(used_s, refs[:those_s]))
        ups = dict(zip(used_s, refs[those_s : 2 * those_s]))
        refs = refs[2 * those_s :]
        grads, (gate, up), refs = refs[:many], refs[many : many + 2], refs[many + 2 :]
        backs, (gate_out, up_out, gate_rows, up_rows) = refs[:many], refs[many:]

        @pl.when(pl.program_id(0) == 0)
        def _():
            for i, (t, those) in enumerate(groups):
                terms = {}
                for d in range(2):
                    for s in those:
                        here = pl.ds((t * 2 + d) * slot, slot)
                        g, u = gates[s][here, :], ups[s][here, :]
                        h = grads[i][pl.ds((d * 4 + s) * slot, slot), :]
                        sig = jax.nn.sigmoid(g)
                        terms[d, s] = (h * u * sig * (1.0 + g * (1.0 - sig)), h * g * sig)
                order = [terms[d, s] for d in range(2) for s in those]
                for which, by_t, by_s in ((0, gate_rows, gate_out), (1, up_rows, up_out)):
                    for k in range(0, len(order), 2):
                        pair = jnp.concatenate([order[k][which], order[k + 1][which]], axis=0)
                        by_t[pl.ds(starts[i] + k * slot, 2 * slot), :] = pair.astype(BF)
                    for s in those:
                        pair = jnp.concatenate([terms[0, s][which], terms[1, s][which]], axis=0)
                        by_s[pl.ds(pairs.index((s, t)) * 2 * slot, 2 * slot), :] = pair.astype(BF)

        back = mm_last(gate_rows[...], gate[...]) + mm_last(up_rows[...], up[...])
        for i in range(many):
            backs[i][...] = back[starts[i] : starts[i] + counts[i]].astype(BF)

    both = jax.ShapeDtypeStruct((total, units), BF)
    operands = [gate_pre[s] for s in used_s] + [up_pre[s] for s in used_s]
    operands += [hidden_grad[t] for t, _ in groups]
    outs = kernel_call(
        body,
        7,
        [whole(a) for a in operands] + [rows_block(n, units)] * 2,
        [columns(count, n) for count in counts] + [whole(both)] * 2,
        [jax.ShapeDtypeStruct((count, width), BF) for count in counts] + [both] * 2,
        [pltpu.VMEM(both.shape, BF)] * 2,
    )(*operands, gate_matrix, up_matrix)
    grads = [
        {pair: a[k * 2 * slot : (k + 1) * 2 * slot] for k, pair in enumerate(pairs)} for a in outs[many:]
    ]
    return outs[:many], grads[0], grads[1]


def local(tokens, grad_out, expert_ids, route_weight, w_gate, w_up, w_down):
    inputs = tokens[0, 0]
    upstream = grad_out[0, 0]
    weights = route_weight[0, 0]
    gate_matrix, up_matrix, down_matrix = w_gate[0, 0], w_up[0, 0], w_down[0, 0]
    experts = lax.axis_size("expert")
    rows, per_token = weights.shape
    width = inputs.shape[1]
    split = rows // 2
    slot = 3 * rows * per_token // (2 * experts)
    flat = 8 * slot
    me = lax.axis_index("expert")
    y, zl, c = me // 4, (me // 2) % 2, me % 2

    ids = expert_ids[0, 0].astype(F32)
    fields = [ids] + [jnp.stack([a[:, k] for a in in_three(weights)], axis=1) for k in range(per_token)]
    fields = jnp.concatenate(fields, axis=1).astype(BF)
    codes = slot_codes(ids, experts, slot)
    step = jnp.arange(4, dtype=jnp.int32)
    two = jnp.arange(2, dtype=jnp.int32)
    slots = jnp.arange(slot, dtype=jnp.int32)
    dest_y = ((y + step) % 4) * 4
    targets_z = (
        (dest_y[None, :, None] + zl * 2 + (c ^ two)[:, None, None]) * slot + slots
    ).reshape(-1)
    targets_y = (
        (
            dest_y[None, :, None, None]
            + (zl ^ two)[None, None, :, None] * 2
            + (c ^ two)[:, None, None, None]
        )
        * slot
        + slots
    ).reshape(-1)
    each_y, pick_y, _ = chosen(codes, weights, targets_y)
    own, sib = [
        mm_first(pick_y[:, dc * flat : (dc + 1) * flat], inputs).astype(BF) for dc in range(2)
    ]
    message = jnp.concatenate(
        [after(upstream, sib), jnp.pad(fields.T, ((0, 0), (0, width - rows)))], axis=0
    )
    near1, near3 = shift_z(message, 1), shift_z(message, 3)
    sib = swap_core(sib)
    along_y = [
        jnp.concatenate([a[t * 2 * slot : (t + 1) * 2 * slot] for a in (own, sib)]) for t in range(4)
    ]
    y1, y3 = shift_y(along_y[1], 1), shift_y(along_y[3], 3)

    near1, near3, y1, y3, far_y = lax.optimization_barrier((near1, near3, y1, y3, along_y[2]))
    y2 = shift_y(far_y, 2)
    far_a, far_b = shift_z(near1[:split], 1), shift_z(near3[split:], 3)
    ring_tables = [fields, near1[rows:, :rows].T, far_b[rows - split :, :rows].T, near3[rows:, :rows].T]

    def picks(table):
        table = table.astype(F32)
        parts = [table[:, per_token + 3 * k : per_token + 3 * k + 3] for k in range(per_token)]
        weigh = jnp.stack([p[:, 0] + p[:, 1] + p[:, 2] for p in parts], axis=-1)
        return chosen(slot_codes(table[:, :per_token], experts, slot), weigh, targets_z)[1:]

    pick_z, slot_weight_z = zip(*[picks(a) for a in ring_tables])
    far_a, far_b, near1, near3, late_upstream = lax.optimization_barrier(
        (far_a, far_b, near1, near3, upstream)
    )
    far = jnp.concatenate([far_a, far_b[: rows - split]])
    sel = [
        (slot_weight_z[s][:, None] * mm_first(pick_z[s], block)).astype(BF).reshape(2, 4, slot, width)
        for s, block in enumerate((late_upstream, near1[:rows], far, near3[:rows]))
    ]
    cross = [jnp.stack([a[1, t] for t in those for a in sel]) for those in ((1, 3), (0, 2))]

    sel, cross, y1, y2, y3 = lax.optimization_barrier((sel, cross, y1, y2, y3))
    by_y = [along_y[0], y1, y2, y3]
    same, other = [
        jnp.concatenate([a[k * slot : (k + 1) * slot] for a in by_y for k in (dl, 2 + dl)])
        for dl in range(2)
    ]
    x1, x3 = shift_z(other, 1), shift_z(other, 3)
    odd, cross_even = lax.optimization_barrier((swap_core(cross[0]), cross[1]))
    even = swap_core(cross_even)
    sib = [even[:4], odd[:4], even[4:], odd[4:]]
    out_y = [
        jnp.concatenate([jnp.stack([sel[s][0, t] for s in range(4)]), sib[t]]).reshape(flat, width)
        for t in range(4)
    ]
    g1, g3 = shift_y(out_y[1], 1), shift_y(out_y[3], 3)

    x1, x3, g1, g3, same_far, out_far = lax.optimization_barrier((x1, x3, g1, g3, same, out_y[2]))
    x2, g2 = shift_z(same_far, 2), shift_y(out_far, 2)
    ahead = forward([x1, x3, same_far], gate_matrix, up_matrix)
    out1, out3 = outputs([ahead[0][2], ahead[1][2]], down_matrix)
    grad1, grad3, grad0 = hidden_grads([g1, g3, out_y[0]], down_matrix)
    gate_pre, up_pre, hidden = [{0: ahead[2][i], 1: ahead[0][i], 3: ahead[1][i]} for i in range(3)]
    early = ((1, (0, 1, 3)), (3, (0, 1, 3)))
    (back1, back3), gate_grad, up_grad = backward(
        early, slot, gate_pre, up_pre, {1: grad1, 3: grad3}, gate_matrix, up_matrix
    )

    x2, g2, out1, out3, back1, back3 = lax.optimization_barrier((x2, g2, out1, out3, back1, back3))
    e1, e3 = shift_z(out1, -1), shift_z(out3, -3)
    b1, b3 = shift_y(back1, -1), shift_y(back3, -3)
    ((gate_pre[2], up_pre[2], hidden[2]),) = forward([x2], gate_matrix, up_matrix)
    (grad2,) = hidden_grads([g2], down_matrix)
    out2, out0 = outputs([hidden[2], hidden[0]], down_matrix)
    rest = ((0, (0, 1, 2, 3)), (2, (0, 1, 2, 3)), (1, (2,)), (3, (2,)))
    (back0, back2, back1, back3), more_gate, more_up = backward(
        rest,
        slot,
        gate_pre,
        up_pre,
        {0: grad0, 1: grad1, 2: grad2, 3: grad3},
        gate_matrix,
        up_matrix,
    )
    gate_grad, up_grad = {**gate_grad, **more_gate}, {**up_grad, **more_up}

    e1, e3, b1, b3, out0, out2, back0, back1, back2, back3 = lax.optimization_barrier(
        (e1, e3, b1, b3, out0, out2, back0, back1, back2, back3)
    )
    e2, b2 = shift_z(out2, -2), shift_y(back2, -2)
    far1, far3 = shift_y(back1, -1), shift_y(back3, -3)
    swapped = swap_core(back0[4 * slot :])
    back0 = back0.reshape(2, 4, slot, width)
    b1, b3 = [a.reshape(2, 3, slot, width) for a in (b1, b3)]
    late_g, late_hidden, _ = lax.optimization_barrier(((out_y[0], g1, g2, g3), hidden, e1))
    late_hidden = jnp.stack([late_hidden[s].reshape(4, 2, slot, -1) for s in range(4)], axis=2)
    down_total = mm_first(late_hidden.reshape(4 * flat, -1), jnp.concatenate(late_g)).astype(BF)

    e1, e2, e3, b2, far1, far3, swapped = lax.optimization_barrier(
        (e1, e2, e3, b2, far1, far3, swapped)
    )
    swapped = swapped.reshape(4, slot, width)
    b2 = b2.reshape(2, 4, slot, width)
    far1, far3 = [a.reshape(2, 1, slot, width) for a in (far1, far3)]
    others = swap_core(jnp.concatenate([b2[1], b1[1], b3[1], far1[1], far3[1]]))

    def in_order(whole0, part1, whole2, part3, rest1, rest3):
        part1, part3 = [[p[0], p[1], r[0], p[2]] for p, r in ((part1, rest1), (part3, rest3))]
        return [whole0, part1, whole2, part3]

    back = [
        in_order(back0[0], b1[0], b2[0], b3[0], far1[0], far3[0]),
        in_order(swapped, others[4:7], others[:4], others[7:10], others[10:11], others[11:]),
    ]

    def by_token(s):
        rows_of = jnp.stack([back[dc][t][s] for dc in range(2) for t in range(4)])
        return mm(pick_z[s], rows_of.reshape(-1, width))

    both = [
        (out0.astype(F32) + e2.astype(F32)).astype(BF).reshape(4, 2, slot, width),
        (e1.astype(F32) + e3.astype(F32)).astype(BF).reshape(4, 2, slot, width),
    ]
    both = [jnp.stack([a[t] for a in both]) for t in range(4)]
    m1, m3 = shift_y(both[1], -1), shift_y(both[3], -3)
    far = by_token(2).astype(BF)
    far_a, far_b = shift_z(far[:split], 1), shift_z(far[split:], -1)
    up_z, down_z, here = by_token(3), by_token(1), by_token(0)

    far_a, far_b, m1, m3, both_far = lax.optimization_barrier((far_a, far_b, m1, m3, both[2]))
    up_z = jnp.concatenate([up_z[:split] + far_a.astype(F32), up_z[split:]]).astype(BF)
    down_z = jnp.concatenate([down_z[:split], down_z[split:] + far_b.astype(F32)]).astype(BF)
    from_down, from_up = shift_z(up_z, 1), shift_z(down_z, -1)
    m2 = shift_y(both_far, -2)
    swapped = swap_core(jnp.stack([both[0][:, 1], m1[:, 1], m3[:, 1]]))
    late_x, late_gate, _ = lax.optimization_barrier(((same, x1, x2, x3), gate_grad, far_a))

    def by_s(grads):
        return jnp.concatenate([grads[s, t] for s in range(4) for t in range(4)])

    late_x = jnp.concatenate(late_x)
    gate_total = mm_first(late_x, by_s(late_gate)).astype(BF)

    sib = [swapped[0], swapped[1], swap_core(m2[:, 1]), swapped[2]]
    back = jnp.stack([both[0][:, 0], m1[:, 0], m2[:, 0], m3[:, 0]] + sib).reshape(-1, width)
    mixed = sum(weights[:, k, None] * mm(each_y[k], back) for k in range(per_token)).astype(BF)
    next_input = from_behind(mixed, "section", 1)
    input_grad = (here + from_down.astype(F32) + from_up.astype(F32)).astype(BF)
    prev_grad = from_behind(input_grad, "section", -1)
    late_x, late_up, _ = lax.optimization_barrier((late_x, up_grad, m2))
    up_total = mm_first(late_x, by_s(late_up)).astype(BF)
    return (
        next_input[None, None],
        prev_grad[None, None],
        gate_total[None, None],
        up_total[None, None],
        down_total[None, None],
    )


def solution(mesh):
    return jax.shard_map(
        local,
        mesh=mesh,
        in_specs=(
            P("section", "dp", "expert", None),
            P("section", "dp", "expert", None),
            P("section", "dp", "expert", None),
            P("section", "dp", "expert", None),
            P("section", "expert", None, "dp"),
            P("section", "expert", None, "dp"),
            P("section", "expert", "dp", None),
        ),
        out_specs=(
            P("section", "dp", "expert", None),
            P("section", "dp", "expert", None),
            P("section", "expert", None, "dp"),
            P("section", "expert", None, "dp"),
            P("section", "expert", "dp", None),
        ),
        check_vma=False,
    )
```
